128 devices in a mesh: pipe: 2 (over core), expert: 16 (over z, x), tensor: 4 (over y).
Axes of the slice: x: 4, y: 4, z: 4, core: 2. Of those that a mesh axis runs over, the one named last changes fastest.
Arguments:
- inputs: bfloat16 [2, 2048, 2048], P(None, 'expert'), may hold values from -6 to 6
- cotangent: bfloat16 [2, 2048, 2048], P(None, 'expert'), may hold values from -6 to 6
- doc_bounds: int32 [2, 16, 2], P(None, 'expert'), may hold values from 1 to 127, as said below
- routes: int32 [2, 2, 2048, 8], P('pipe', None, 'expert'), may hold values from 0 to 31, all different within a row; in each aligned block of 128 rows (0 to 127, 128 to 255, ..., all dimensions but the last counted through in order) at most 48 rows name the same one
- gates: float32 [2, 2, 2048, 8], P('pipe', None, 'expert'), may hold values from 0.06 to 0.25
- norm_attn: float32 [2, 2048], P('pipe'), may hold values from 0.1 to 1.9
- norm_moe: float32 [2, 2048], P('pipe'), may hold values from 0.1 to 1.9
- q_gain: float32 [2, 128], P('pipe'), may hold values from 0.1 to 1.9
- k_gain: float32 [2, 128], P('pipe'), may hold values from 0.1 to 1.9
- w_query: bfloat16 [2, 2048, 4096], P('pipe', 'expert', 'tensor'), may hold values from -0.125 to 0.125
- key_matrix: bfloat16 [2, 2048, 512], P('pipe', 'expert', 'tensor'), may hold values from -0.125 to 0.125
- value_matrix: bfloat16 [2, 2048, 512], P('pipe', 'expert', 'tensor'), may hold values from -0.125 to 0.125
- w_out: bfloat16 [2, 4096, 2048], P('pipe', 'tensor', 'expert'), may hold values from -0.5 to 0.5
- w_gate: bfloat16 [2, 32, 768, 2048], P('pipe', 'expert', 'tensor'), may hold values from -0.125 to 0.125
- w_up: bfloat16 [2, 32, 768, 2048], P('pipe', 'expert', 'tensor'), may hold values from -0.125 to 0.125
- w_down: bfloat16 [2, 32, 768, 2048], P('pipe', 'expert', 'tensor'), may hold values from -0.875 to 0.875
Outputs:
- activations: float32 [2, 2, 2048, 2048], P('pipe', None, 'expert')
- input_grads: float32 [2, 2, 2048, 2048], P('pipe', None, 'expert')
- d_norm_attn: float32 [2, 2048], P('pipe')
- d_norm_moe: float32 [2, 2048], P('pipe')
- d_q_gain: float32 [2, 128], P('pipe')
- d_k_gain: float32 [2, 128], P('pipe')
- d_query: float32 [2, 2048, 4096], P('pipe', 'expert', 'tensor')
- d_key: float32 [2, 2048, 512], P('pipe', 'expert', 'tensor')
- d_value: float32 [2, 2048, 512], P('pipe', 'expert', 'tensor')
- d_out: float32 [2, 4096, 2048], P('pipe', 'tensor', 'expert')
- d_gate_w: float32 [2, 32, 768, 2048], P('pipe', 'expert', 'tensor')
- d_up_w: float32 [2, 32, 768, 2048], P('pipe', 'expert', 'tensor')
- d_down_w: float32 [2, 32, 768, 2048], P('pipe', 'expert', 'tensor')
- d_gates: float32 [2, 2, 2048, 8], P('pipe', None, 'expert')
The draws below stay inside these ranges and needn't reach their ends.
Inputs may be any that keep to these rules, and one draw needn't show every extreme that they name: `routes`: in each aligned block of 128 rows (one group of one layer and micro-batch) no expert is named by more than 48 rows; a row names 8 different experts. `doc_bounds`: each pair (s, e) has s < 64 < e, so that a group holds three documents.
All inputs are finite; a program needn't handle non-finite values.
Results may differ from the reference program's by a relative error of at most 0.03.
Values may be sent and summed in bfloat16 or wider, within the bound.
A program may use at most 320 MiB of HBM per device.

```python
import math
import jax
import jax.numpy as jnp
import numpy as np
from jax import lax

MODEL_DIM = 2048
QUERY_HEADS = 32
KEY_VALUE_HEADS = 4
HEAD_SIZE = 128
FFE = 768
TOPK = 8
ROWS = 128
MICRO = 2
EXPERTS = 32
CAP = 48
GROUPS = 16
TOKENS = 2048
N_PIPE = 2
N_TENSOR = 4


def draw_doc_bounds(key, part):
    key = jax.random.fold_in(key, 7)
    start_key, end_key = jax.random.split(key)
    doc_start = jax.random.randint(start_key, (MICRO, GROUPS), 1, ROWS // 2)
    doc_end = jax.random.randint(end_key, (MICRO, GROUPS), ROWS // 2 + 1, ROWS)
    return jnp.stack([doc_start, doc_end], axis=-1).astype(jnp.int32)


def shard_levels(own_key, extent, shards, least, largest):
    level = 1.0
    for position, shards_of in shards:
        draws = jax.random.uniform(jax.random.fold_in(jax.random.fold_in(own_key, 6), position), (shards_of,), jnp.float32, least / len(shards), largest / len(shards))
        level = level * jnp.repeat(jnp.exp(draws), extent[position] // shards_of).reshape((-1,) + (1,) * (len(extent) - 1 - position))
    return level


def assign_block(key, own, number, rows, count, top, most, slope):
    ranking = jax.random.permutation(key, count)
    crowded, ordinary = load_shares(count, rows * top, most, slope, True), load_shares(count, rows * top, most, slope, False)
    places = jnp.arange(count)

    def named(lengths, offset_by):
        used = int((lengths > 0).sum())
        fixed = max(1, used // 4)
        moved = fixed + (places - fixed + offset_by * (used - fixed)) % max(1, count - fixed)
        return jnp.zeros((count,), jnp.int32).at[ranking[jnp.where(places < fixed, places, moved)]].set(jnp.asarray(lengths, jnp.int32))

    lengths = jnp.where(number % 4 == 0, named(crowded, number // 4), named(ordinary, number - number // 4 - 1))
    mixed = jax.random.permutation(jax.random.fold_in(own, 3), count)
    source_of, receiver = mixed[0:count // 2 * 2:2], mixed[1:count // 2 * 2:2]
    slack = jnp.minimum(lengths[source_of] - 1, most - lengths[receiver]) // 2
    slack = jnp.where((source_of == ranking[0]) | (receiver == ranking[0]) | (lengths[receiver] == 0), 0, jnp.maximum(slack, 0))
    moved = jax.random.randint(jax.random.fold_in(own, 4), (count // 2,), 0, 1 << 20) % (slack + 1)
    lengths = lengths.at[source_of].add(-moved).at[receiver].add(moved)
    members = jnp.searchsorted(jnp.cumsum(lengths), jnp.arange(rows * top), side="right").astype(jnp.int32)
    table = members.reshape(top, rows).T
    table = table[jax.random.permutation(jax.random.fold_in(own, 1), rows)]
    offset_by = jax.random.randint(jax.random.fold_in(own, 2), (rows, 1), 0, top)
    return jnp.take_along_axis(table, (jnp.arange(top)[None, :] + offset_by) % top, axis=1)


def load_shares(number_of, total, bound, lean, full):
    loads = [(1 << 20) // math.isqrt(standing ** lean) + 1 for standing in range(1, number_of + 1)]
    largest = bound if full else min(bound, max(-(-total // number_of), total * loads[0] // sum(loads)))
    least = 1 if total - largest >= number_of - 1 else 0
    given, spare = [largest] + [least] * (number_of - 1), total - largest - least * (number_of - 1)
    while spare > 0:
        free = [i for i in range(1, number_of) if given[i] < largest] or [i for i in range(1, number_of) if given[i] < bound]
        pool, remaining = sum([loads[i] for i in free]), spare
        for i in free:
            more = min(bound - given[i], max(1, remaining * loads[i] // pool), spare)
            given[i] = given[i] + more
            spare = spare - more
    return np.array(given)


def gaussian(stream_key, shape, scale, most, cuts=(), held_as=jnp.bfloat16):
    level = shard_levels(stream_key, shape, cuts, -0.22, 0.18) if cuts else 1.0
    drawn = jax.random.normal(stream_key, shape, jnp.float32) * scale * level
    return jnp.minimum(jnp.maximum(drawn, -most), most).astype(held_as)


def setup_inputs(seed: int = 0) -> dict:
    key_list = jax.random.split(jax.random.key(seed), 17)
    inputs = gaussian(key_list[0], (MICRO, TOKENS, MODEL_DIM), 1.0, 6.0, ((1, 16),))
    cotangent = gaussian(key_list[1], (MICRO, TOKENS, MODEL_DIM), 1.0, 6.0, ((1, 16),))
    doc_bounds = draw_doc_bounds(jax.random.fold_in(key_list[16], 71), 0)
    routes_keys = jax.random.split(jax.random.fold_in(key_list[3], 1), N_PIPE * MICRO * TOKENS // ROWS)
    routes_turns = jax.random.permutation(jax.random.fold_in(key_list[3], 3), N_PIPE * MICRO * TOKENS // ROWS)
    routes = jax.vmap(lambda own, number: assign_block(jax.random.fold_in(key_list[3], 2), own, number, ROWS, EXPERTS, TOPK, CAP, 2))(routes_keys, routes_turns).reshape((N_PIPE, MICRO, TOKENS, TOPK))
    gates = jnp.clip(jnp.exp(math.log(0.25) - 1.4271164 * jax.random.uniform(key_list[4], (N_PIPE, MICRO, TOKENS, TOPK), jnp.float32) ** shard_levels(key_list[4], (N_PIPE, MICRO, TOKENS, TOPK), ((0, 2), (2, 16)), -0.2, 0.2)), 0.06, 0.25)
    norm_attn = jnp.clip(1.0 + 0.18 * jax.random.normal(key_list[5], (N_PIPE, MODEL_DIM), jnp.float32), 0.1, 1.9)
    norm_moe = jnp.clip(1.0 + 0.18 * jax.random.normal(key_list[6], (N_PIPE, MODEL_DIM), jnp.float32), 0.1, 1.9)
    q_gain = jnp.clip(1.0 + 0.18 * jax.random.normal(key_list[7], (N_PIPE, HEAD_SIZE), jnp.float32), 0.1, 1.9)
    k_gain = jnp.clip(1.0 + 0.18 * jax.random.normal(key_list[8], (N_PIPE, HEAD_SIZE), jnp.float32), 0.1, 1.9)
    w_query = gaussian(key_list[9], (N_PIPE, MODEL_DIM, QUERY_HEADS * HEAD_SIZE), MODEL_DIM ** -0.5, 0.125, ((0, 2), (1, 16), (2, 4)))
    key_matrix = gaussian(key_list[10], (N_PIPE, MODEL_DIM, KEY_VALUE_HEADS * HEAD_SIZE), MODEL_DIM ** -0.5, 0.125, ((0, 2), (1, 16), (2, 4)))
    value_matrix = gaussian(key_list[11], (N_PIPE, MODEL_DIM, KEY_VALUE_HEADS * HEAD_SIZE), MODEL_DIM ** -0.5, 0.125, ((0, 2), (1, 16), (2, 4)))
    w_out = gaussian(key_list[12], (N_PIPE, QUERY_HEADS * HEAD_SIZE, MODEL_DIM), (QUERY_HEADS * HEAD_SIZE // 32) ** -0.5, 0.5, ((0, 2), (1, 4), (2, 16)))
    w_gate = gaussian(key_list[13], (N_PIPE, EXPERTS, FFE, MODEL_DIM), MODEL_DIM ** -0.5, 0.125, ((0, 2), (1, 16), (2, 4)))
    w_up = gaussian(key_list[14], (N_PIPE, EXPERTS, FFE, MODEL_DIM), MODEL_DIM ** -0.5, 0.125, ((0, 2), (1, 16), (2, 4)))
    w_down = gaussian(key_list[15], (N_PIPE, EXPERTS, FFE, MODEL_DIM), (FFE // 16) ** -0.5, 0.875, ((0, 2), (1, 16), (2, 4)))
    return {"inputs": inputs, "cotangent": cotangent, "doc_bounds": doc_bounds, "routes": routes, "gates": gates, "norm_attn": norm_attn, "norm_moe": norm_moe, "q_gain": q_gain, "k_gain": k_gain, "w_query": w_query, "key_matrix": key_matrix, "value_matrix": value_matrix, "w_out": w_out, "w_gate": w_gate, "w_up": w_up, "w_down": w_down}


@jax.custom_vjp
def reduced_precision(v):
    return lax.optimization_barrier(v.astype(jnp.bfloat16)).astype(jnp.float32)

@jax.custom_vjp
def reduced_backward(v):
    return v

def low_keep(v):
    return (reduced_precision(v), None)

def low_pass(kept, grad):
    return (grad,)

def back_keep(v):
    return (v, None)

def back_low(kept, grad):
    return (reduced_precision(grad),)
reduced_precision.defvjp(low_keep, low_pass)
reduced_backward.defvjp(back_keep, back_low)
eps = 1e-06
rope_base = 1000000.0
highest = lax.Precision.HIGHEST

def matrix_product(left, right):
    return jnp.dot(left, right, precision=highest, preferred_element_type=jnp.float32)

def rms_scale(values):
    return lax.rsqrt(lax.optimization_barrier(jnp.mean(values * values, axis=-1, keepdims=True)) + eps)

def rotary(values, cosine, sine_table):
    half_width = values.shape[-1] // 2
    lower_half = values[..., :half_width]
    upper_half = values[..., half_width:]
    return jnp.concatenate([lower_half * cosine - upper_half * sine_table, upper_half * cosine + lower_half * sine_table], axis=-1)

def rotary_tables(positions, head_width):
    freqs = rope_base ** (-(2.0 * jnp.arange(head_width // 2, dtype=jnp.float32)) / head_width)
    angles = positions[:, None] * freqs[None, :]
    return (jnp.cos(angles)[:, None, :], jnp.sin(angles)[:, None, :])

def doc_layout(bounds, rows_total):
    row_place = jnp.arange(rows_total, dtype=jnp.int32)
    doc_start = bounds[0]
    doc_end = bounds[1]
    segment_piece = (row_place >= doc_start).astype(jnp.int32) + (row_place >= doc_end).astype(jnp.int32)
    first_place = jnp.where(segment_piece == 0, 0, jnp.where(segment_piece == 1, doc_start, doc_end)).astype(jnp.int32)
    return (segment_piece, (row_place - first_place).astype(jnp.float32))

def slot_layout(route_rows, expert_count, capacity):
    rows_total, top_count = route_rows.shape
    onehot = (route_rows[:, :, None] == jnp.arange(expert_count, dtype=jnp.int32)[None, None, :]).astype(jnp.int32)
    per_row = lax.optimization_barrier(jnp.sum(onehot, axis=1, dtype=jnp.int32))
    before = jnp.cumsum(per_row, axis=0, dtype=jnp.int32) - per_row
    slot = lax.optimization_barrier(jnp.sum(onehot * before[:, None, :], axis=2, dtype=jnp.int32))
    slot_index = (route_rows * capacity + slot).astype(jnp.int32)
    slot_owner = jnp.full((expert_count * capacity,), rows_total * top_count, jnp.int32)
    slot_owner = slot_owner.at[slot_index.reshape(-1)].set(jnp.arange(rows_total * top_count, dtype=jnp.int32))
    return (slot_index, slot_owner)

def grouped_query_attention(query_rotated, key_rotated, value_flat, segment_piece):
    rows_total, head_count, head_width = query_rotated.shape
    kv_count = key_rotated.shape[1]
    grouped = query_rotated.reshape(rows_total, kv_count, head_count // kv_count, head_width)
    scores = reduced_backward(jnp.einsum('rkgd,skd->kgrs', grouped, key_rotated, precision=highest) * head_width ** (-0.5))
    row_place = jnp.arange(rows_total)
    allowed = (segment_piece[:, None] == segment_piece[None, :]) & (row_place[None, :] <= row_place[:, None])
    scores = jnp.where(allowed, scores, -1e+30)
    row_peak = lax.optimization_barrier(jnp.max(scores, axis=-1, keepdims=True))
    weights = jnp.exp(scores - row_peak)
    probs_r = reduced_precision(weights / lax.optimization_barrier(jnp.sum(weights, axis=-1, keepdims=True)))
    mixed_output = jnp.einsum('kgrs,skd->rkgd', probs_r, value_flat, precision=highest)
    return mixed_output.reshape(rows_total, head_count * head_width)

def expert_rows(slot_rows, gate_w, up_w, down_w):
    summed = jnp.zeros(slot_rows.shape, jnp.float32)
    block_width = gate_w.shape[0] // N_TENSOR
    for block_number in range(N_TENSOR):
        window = slice(block_number * block_width, (block_number + 1) * block_width)
        local_rows = reduced_backward(slot_rows)
        gate_v = reduced_backward(matrix_product(local_rows, gate_w[window, :].T))
        up_v = reduced_backward(matrix_product(local_rows, up_w[window, :].T))
        hidden = reduced_precision(jax.nn.silu(gate_v) * up_v)
        summed = summed + reduced_backward(reduced_precision(matrix_product(hidden, down_w[window, :])))
    return summed

def layer(state, gain_set, weight_set, route_rows, gate_rows, bounds):
    norm_attn, norm_moe, q_gain, k_gain = gain_set
    w_query, key_matrix, value_matrix, w_out, w_gate, w_up, w_down = weight_set
    tokens_total = state.shape[0]
    groups_total = bounds.shape[0]
    rows_total = tokens_total // groups_total
    segment_piece, positions = jax.vmap(lambda pair: doc_layout(pair, rows_total))(bounds)
    normalized_input = reduced_precision(state * rms_scale(state) * norm_attn)
    query_f = reduced_backward(matrix_product(normalized_input, w_query)).reshape(tokens_total, QUERY_HEADS, HEAD_SIZE)
    key_flat = reduced_backward(matrix_product(normalized_input, key_matrix)).reshape(tokens_total, KEY_VALUE_HEADS, HEAD_SIZE)
    value_flat = reduced_backward(reduced_precision(matrix_product(normalized_input, value_matrix))).reshape(tokens_total, KEY_VALUE_HEADS, HEAD_SIZE)
    cosine, sine_table = rotary_tables(positions.reshape(-1), HEAD_SIZE)
    query_rotated = reduced_precision(rotary(query_f * rms_scale(query_f) * q_gain, cosine, sine_table))
    key_rotated = reduced_precision(rotary(key_flat * rms_scale(key_flat) * k_gain, cosine, sine_table))
    mixed_output = lax.map(jax.checkpoint(lambda packed_rows: grouped_query_attention(*packed_rows)), (query_rotated.reshape(groups_total, rows_total, QUERY_HEADS, HEAD_SIZE), key_rotated.reshape(groups_total, rows_total, KEY_VALUE_HEADS, HEAD_SIZE), value_flat.reshape(groups_total, rows_total, KEY_VALUE_HEADS, HEAD_SIZE), segment_piece))
    attended = reduced_backward(reduced_precision(mixed_output.reshape(tokens_total, QUERY_HEADS * HEAD_SIZE)))
    middle = state + reduced_backward(matrix_product(attended, w_out))
    moe_in = reduced_precision(middle * rms_scale(middle) * norm_moe)
    route_groups = route_rows.reshape(groups_total, rows_total, TOPK)
    slot_index, slot_owner = jax.vmap(lambda rows_in: slot_layout(rows_in, EXPERTS, CAP))(route_groups)
    extended = jnp.concatenate([moe_in.reshape(groups_total, rows_total, MODEL_DIM), jnp.zeros((groups_total, 1, MODEL_DIM), jnp.float32)], axis=1)
    picked = jax.vmap(lambda table, owners: table[owners // TOPK])(extended, slot_owner)
    picked = picked.reshape(groups_total, EXPERTS, CAP, MODEL_DIM).transpose(1, 0, 2, 3).reshape(EXPERTS, groups_total * CAP, MODEL_DIM)
    returned = lax.map(jax.checkpoint(lambda packed_rows: expert_rows(*packed_rows)), (picked, w_gate, w_up, w_down))
    returned = returned.reshape(EXPERTS, groups_total, CAP, MODEL_DIM).transpose(1, 0, 2, 3).reshape(groups_total, EXPERTS * CAP, MODEL_DIM)
    chosen = jax.vmap(lambda table, places: table[places])(returned, slot_index)
    mixture = jnp.einsum('grk,grkd->grd', gate_rows.reshape(groups_total, rows_total, TOPK), chosen, precision=highest)
    return middle + mixture.reshape(tokens_total, MODEL_DIM)

def reference(inputs, cotangent, doc_bounds, routes, gates, norm_attn, norm_moe, q_gain, k_gain, w_query, key_matrix, value_matrix, w_out, w_gate, w_up, w_down):
    weight_set = tuple((weight.astype(jnp.float32) for weight in (w_query, key_matrix, value_matrix, w_out, w_gate, w_up, w_down)))
    gain_set = (norm_attn, norm_moe, q_gain, k_gain)
    begin = inputs.astype(jnp.float32)
    nudge = jnp.zeros(begin.shape, jnp.float32)

    def forward(begin, nudge, gain_set, weight_set, gate_all):
        firsts = []
        seconds = []
        for batch_number in range(MICRO):
            first_out = layer(begin[batch_number], tuple((gain[0] for gain in gain_set)), tuple((weight[0] for weight in weight_set)), routes[0, batch_number], gate_all[0, batch_number], doc_bounds[batch_number])
            handed = reduced_backward(reduced_precision(first_out)) + nudge[batch_number]
            second_out = layer(handed, tuple((gain[1] for gain in gain_set)), tuple((weight[1] for weight in weight_set)), routes[1, batch_number], gate_all[1, batch_number], doc_bounds[batch_number])
            firsts.append(first_out)
            seconds.append(second_out)
        return (jnp.stack(seconds), jnp.stack(firsts))
    finals, pullback, firsts = jax.vjp(forward, begin, nudge, gain_set, weight_set, gates, has_aux=True)
    d_begin, d_nudge, d_gain_set, d_weight_set, d_gate_all = pullback(cotangent.astype(jnp.float32))
    activations = jnp.stack([firsts, finals])
    input_grads = jnp.stack([d_begin, d_nudge])
    return (activations, input_grads, d_gain_set[0], d_gain_set[1], d_gain_set[2], d_gain_set[3], d_weight_set[0], d_weight_set[1], d_weight_set[2], d_weight_set[3], d_weight_set[4], d_weight_set[5], d_weight_set[6], d_gate_all)
```

```python
import functools
import math

import jax
import jax.numpy as jnp
from jax import lax
from jax.experimental import pallas as pl
from jax.experimental.pallas import tpu as pltpu
from jax.sharding import PartitionSpec as P

MESH = pl.DeviceIdType.MESH
ANY = pl.ANY
VM = pltpu.VMEM
F32 = jnp.float32
BF = jnp.bfloat16

HEAD_SIZE = 128
TOPK = 8
RING = 4
ROWS = 128
OWN = 32
WIDTH = 2048
HIDDEN = 384
QKV = 1280
ATT = 2304
EXPERTS = 32
GAIN_ROWS = 40
eps = 1e-06
rope_base = 1000000.0

ORDERS = (("y", "x", "z"), ("x", "z", "y"), ("z", "y", "x"))
CUTS = (
    ((0, 768), (768, 640), (1408, 640)),
    ((0, 640), (640, 768), (1408, 640)),
)
WORDERS = (("x", "z"), ("z", "x"))
WCUTS = ((0, 1152), (1152, 1152))


class Tile:
    def __init__(self, r0, rows, c0, cols, by_rows):
        self.r0, self.rows, self.c0, self.cols, self.by_rows = r0, rows, c0, cols, by_rows
        if by_rows:
            first = rows // 2
            self.spans = {
                None: (0, rows, 0, cols),
                0: (0, first, 0, cols),
                1: (first, rows - first, 0, cols),
            }
        else:
            first = (cols // 128 + 1) // 2 * 128
            self.spans = {
                None: (0, rows, 0, cols),
                0: (0, rows, 0, first),
                1: (0, rows, first, cols - first),
            }

    def shape(self, half=None):
        _, rows, _, cols = self.spans[half]
        return (rows, cols)

    def at(self, half=None):
        r, rows, c, cols = self.spans[half]
        return (pl.ds(self.r0 + r, rows), pl.ds(self.c0 + c, cols))

    def own(self):
        return Tile(0, self.rows, 0, self.cols, self.by_rows)


class Place:
    def __init__(self):
        self.pipe = lax.axis_index("pipe")
        expert = lax.axis_index("expert")
        self.at = {
            "z": lax.div(expert, RING),
            "x": lax.rem(expert, RING),
            "y": lax.axis_index("tensor"),
        }

    def step(self, axis, by):
        return lax.rem(self.at[axis] + (by + RING), RING)

    def device(self, axis, by):
        at = dict(self.at)
        at[axis] = self.step(axis, by)
        return (self.pipe, at["z"] * RING + at["x"], at["y"])

    def sibling(self):
        return (1 - self.pipe, self.at["z"] * RING + self.at["x"], self.at["y"])


class Net:
    def __init__(self, send, recv, base=0):
        self.send, self.recv, self.base, self.made = send, recv, base, []

    def describe(self, src, dst, device, i):
        return pltpu.make_async_remote_copy(
            src_ref=src,
            dst_ref=dst,
            send_sem=self.send.at[self.base + i],
            recv_sem=self.recv.at[self.base + i],
            device_id=device,
            device_id_type=MESH,
        )

    def copy(self, src, dst, device):
        made = self.describe(src, dst, device, len(self.made))
        made.start()
        self.made.append(made)
        return made

    def finish(self):
        for made in self.made:
            made.wait_send()


def greet(devices, before_wait=None):
    barrier = pltpu.get_barrier_semaphore()
    for device in devices:
        pl.semaphore_signal(barrier, inc=1, device_id=device, device_id_type=MESH)
    wait_loads()
    if before_wait is not None:
        before_wait()
    pl.semaphore_wait(barrier, len(devices))


def greet_sibling(place, devices, before_wait):
    barrier = pltpu.get_barrier_semaphore()
    for device in devices:
        pl.semaphore_signal(barrier, inc=1, device_id=device, device_id_type=MESH)

    @pl.when(place.pipe == 0)
    def _():
        pl.semaphore_signal(barrier, inc=1, device_id=place.sibling(), device_id_type=MESH)

    wait_loads()
    before_wait()

    @pl.when(place.pipe == 0)
    def _():
        pl.semaphore_wait(barrier, len(devices))

    @pl.when(place.pipe == 1)
    def _():
        pl.semaphore_wait(barrier, len(devices) + 1)


def around(place, axes):
    return [place.device(axis, by) for axis in axes for by in (1, -1)]


def together(steps):
    for _ in in_turn(steps):
        pass


def in_turn(steps):
    live = list(steps)
    while live:
        kept = []
        for step in live:
            try:
                next(step)
                kept.append(step)
            except StopIteration:
                pass
        live = kept
        if live:
            yield


def gather_ring(net, place, axis, block, first=None, seen=None):
    me, left, right, far = (place.step(axis, by) for by in (0, -1, 1, 2))
    mine = block(me, None) if first is None else first
    to_right = net.copy(mine, block(me, None), place.device(axis, 1))
    to_left = net.copy(mine, block(me, None), place.device(axis, -1))
    yield
    to_right.wait_recv()
    on_right = net.copy(block(left, 0), block(left, 0), place.device(axis, 1))
    to_left.wait_recv()
    on_left = net.copy(block(right, 1), block(right, 1), place.device(axis, -1))
    if seen is not None:
        seen(left)
        seen(right)
    yield
    on_right.wait_recv()
    on_left.wait_recv()
    if seen is not None:
        seen(far)


def gather_all(net, place, order, block, first):
    wanted = {axis: place.at[axis] for axis in order}
    for number, axis in enumerate(order):
        held = dict(wanted)

        def part(i, half, held=held, axis=axis):
            return block({**held, axis: i}, half)

        yield from gather_ring(net, place, axis, part, first if number == 0 else None)
        wanted[axis] = None


SUBS = [(chunk, sub) for chunk in range(3) for sub in range(2)]
TILES = {
    (chunk, sub): Tile(sub * 16, 16, *CUTS[sub][chunk], False) for chunk, sub in SUBS
}
TALLY_TILE = Tile(0, OWN, 0, 128, True)
STATE_TILES = [Tile(lo, 16, 0, WIDTH, False) for lo in (0, 16)]
WSUBS = [(chunk, sub) for chunk in range(2) for sub in range(2)]
WTILES = {
    (chunk, sub): Tile(sub * 64, 64, WCUTS[chunk][0], WCUTS[chunk][1], True)
    for chunk, sub in WSUBS
}


def add_into(out, terms, shape):
    def tile(spot):
        summed = terms[0][spot]
        for term in terms[1:]:
            summed = summed + term[spot]
        out[spot] = summed

    lead, rows = shape[:-2], shape[-2]
    if len(lead) == 2:

        def each(i, _):
            tile((i, slice(None), slice(None), slice(None)))
            return 0

        lax.fori_loop(0, lead[0], each, 0)
    elif rows <= OWN:
        tile((slice(None),) * len(shape))
    else:
        tiles = rows // OWN

        def each(i, _):
            spot = (pl.ds(pl.multiple_of(lax.rem(i, tiles) * OWN, OWN), OWN), slice(None))
            tile((lax.div(i, tiles),) * len(lead) + spot)
            return 0

        lax.fori_loop(0, tiles * (lead[0] if lead else 1), each, 0)


def ring_scratch(lead, tile):
    return [
        VM(lead + tile.shape(0), BF),
        VM(lead + tile.shape(1), BF),
        VM(lead + tile.shape(), BF),
        VM(lead + tile.shape(), BF),
    ]


def reduce_ring(net, place, axis, block, lead, tile, bufs, make=None):
    near_left, near_right, from_left, from_right = bufs
    whole = (slice(None),) * len(lead)

    def half_of(ref, half):
        return ref.at[whole + tile.own().at(half)]

    me, left, right, far = (place.step(axis, by) for by in (0, -1, 1, 2))
    go_right, go_left = place.device(axis, 1), place.device(axis, -1)
    if make is not None:
        make(2)
    far_right = net.copy(block(far, 0), near_left, go_right)
    far_left = net.copy(block(far, 1), near_right, go_left)
    if make is not None:
        yield
        make(1)
    own_right = net.copy(block(right, 1), half_of(from_left, 1), go_right)
    if make is not None:
        make(-1)
    own_left = net.copy(block(left, 0), half_of(from_right, 0), go_left)
    yield
    far_right.wait_recv()
    add_into(near_left, [near_left, block(right, 0)], lead + tile.shape(0))
    sum_right = net.copy(near_left, half_of(from_left, 0), go_right)
    far_left.wait_recv()
    add_into(near_right, [near_right, block(left, 1)], lead + tile.shape(1))
    sum_left = net.copy(near_right, half_of(from_right, 1), go_left)
    yield
    if make is not None:
        make(0)
    for made in (own_right, sum_right, own_left, sum_left):
        made.wait_recv()
    add_into(from_left, [from_left, block(me, None), from_right], lead + tile.shape())


def reduce_all(net, place, order, names, source, tile, bufs, make=None):
    left = [name for name in names]
    for number, axis in enumerate(order):
        spot = left.index(axis)
        lead = tuple(RING for _ in left[1:])
        if number == 0:
            block = lambda i, half, axis=axis: source({axis: i}, half)
        else:
            prior = bufs[number - 1][2]

            def block(i, half, prior=prior, spot=spot, count=len(left)):
                where = [slice(None)] * count
                where[spot] = i
                return prior.at[tuple(where) + tile.own().at(half)]

        yield from reduce_ring(
            net, place, axis, block, lead, tile, bufs[number], make if number == 0 else None
        )
        left.remove(axis)


def reduce_scratch(order_count, tile):
    return [
        ring_scratch((RING,) * (order_count - 1 - number), tile) for number in range(order_count)
    ]


def take(refs, structure):
    return [take(refs, part) if isinstance(part, list) else refs.pop(0) for part in structure]


def flat(structure):
    return [leaf for part in structure for leaf in (flat(part) if isinstance(part, list) else [part])]


def token_block(ref, tile):
    def block(wanted, half):
        where = tuple(slice(None) if wanted.get(a) is None else wanted[a] for a in ("z", "x", "y"))
        return ref.at[where + tile.at(half)]

    return block


def gather_tokens(net, place, stream, own, out):
    return in_turn(
        [
            gather_all(
                net,
                place,
                ORDERS[chunk],
                token_block(out, TILES[chunk, stream]),
                own.at[TILES[chunk, stream].at()],
            )
            for chunk in range(3)
        ]
    )


def inv_rms(values):
    return lax.rsqrt(jnp.mean(values * values, axis=-1, keepdims=True) + eps)


def tensor_blocks(ref, tile):
    def block(i, half):
        return ref.at[(i,) + tile.at(half)]

    return block


def reduce_tensor(net, place, stream, part, bufs):
    tile = STATE_TILES[stream]
    return reduce_ring(net, place, "y", tensor_blocks(part, tile), (), tile, bufs[stream])


def gather_tensor(net, place, stream, held):
    return gather_ring(net, place, "y", tensor_blocks(held, STATE_TILES[stream]))


def state_scratch():
    return flat([ring_scratch((), tile) for tile in STATE_TILES])


def state_bufs(refs):
    return take(list(refs), [[None] * 4, [None] * 4])


def norm_back(dy, values, gain):
    scale = inv_rms(values)
    weighted = dy * gain
    back = scale * weighted - values * (scale * scale * scale) * jnp.mean(
        weighted * values, axis=-1, keepdims=True
    )
    return back, dy * values * scale


TOKENS_ALL = (RING, RING, RING, OWN, WIDTH)
GATHER_COPIES = 4 * 9 * 2
REDUCE_COPIES = 6 * 9 * 2


class Load:
    def __init__(self, shape=None, pick=None):
        self.shape, self.pick = shape, pick or (lambda ref: ref)


LOAD = Load()
LOADING = []


def wait_loads():
    while LOADING:
        LOADING.pop().wait()


def loading(kernel, kinds, args):
    loads = [i for i, kind in enumerate(kinds) if isinstance(kind, Load)]
    scratch = [VM(kinds[i].shape or args[i].shape, args[i].dtype) for i in loads]
    scratch.append(pltpu.SemaphoreType.DMA((len(loads),)))

    def wrapped(*refs):
        refs, held, sems = list(refs[: -len(loads) - 1]), refs[-len(loads) - 1 : -1], refs[-1]
        for k, i in enumerate(loads):
            made = pltpu.make_async_copy(kinds[i].pick(refs[i]), held[k], sems.at[k])
            made.start()
            LOADING.append(made)
            refs[i] = held[k]
        kernel(*refs)

    return wrapped, scratch, [ANY if isinstance(kind, Load) else kind for kind in kinds]


def call(kernel, ident, shapes, in_kinds, out_kinds, scratch, args, copies, vmem=60):
    kernel, held, in_kinds = loading(kernel, in_kinds, args)
    return pl.pallas_call(
        kernel,
        out_shape=shapes,
        in_specs=[pl.BlockSpec(memory_space=kind) for kind in in_kinds],
        out_specs=[pl.BlockSpec(memory_space=kind) for kind in out_kinds],
        scratch_shapes=scratch
        + [pltpu.SemaphoreType.DMA((copies,)), pltpu.SemaphoreType.DMA((copies,))]
        + held,
        compiler_params=pltpu.CompilerParams(
            collective_id=ident, has_side_effects=True, vmem_limit_bytes=vmem * 2**20
        ),
    )(*args)


def of_pipe(ref):
    return ref.at[lax.axis_index("pipe")]


def with_sem(kernel):
    def inner(*refs):
        return kernel(*refs[:-3], refs[-2], refs[-1], refs[-3])

    return inner


def reduce_tokens(net, place, stream, part, bufs, make):
    return in_turn(
        [
            reduce_all(
                net,
                place,
                ORDERS[chunk][::-1],
                ("z", "x", "y"),
                token_block(part, TILES[chunk, stream]),
                TILES[chunk, stream],
                bufs[chunk, stream],
                functools.partial(make, chunk, stream),
            )
            for chunk in range(3)
        ]
    )


def token_scratch():
    return flat([reduce_scratch(3, TILES[sub]) for sub in SUBS])


def token_bufs(refs):
    return {sub: [[refs.pop(0) for _ in range(4)] for _ in range(3)] for sub in SUBS}


def token_sums(bufs, sub):
    return jnp.concatenate(
        [bufs[chunk, sub][-1][2][...].astype(F32) for chunk in range(3)], axis=-1
    )


def add_rows(out, rows):
    out[...] = out[...] + jnp.sum(rows, axis=0, keepdims=True)


def state_back(place, stream, base, dmid, gain, bufs, dgain, put):
    t = place.at["y"]
    rs = pl.ds(stream * 16, 16)
    summed = bufs[stream][2][...].astype(F32)
    back, rows = norm_back(summed, base[t, rs, :].astype(F32), gain[...])
    put(t, rs, (dmid[rs, :] + back).astype(BF))
    add_rows(dgain, rows)


def run_schedule(schedule, steps):
    for name in schedule:
        next(steps[name], None)
    together(steps.values())


DENSE_COPIES = 16
RING_COPIES = 32
PASS_COPIES = 28


def write_tables(bounds, pipe, cosine, sine, bias):
    start, end = bounds[pipe, 0, 0], bounds[pipe, 0, 1]
    row = lax.broadcasted_iota(jnp.int32, (ROWS, 128), 0)
    lane = lax.broadcasted_iota(jnp.int32, (ROWS, 128), 1)
    first = jnp.where(row >= end, end, jnp.where(row >= start, start, 0))
    past = jnp.where(row >= end, ROWS, jnp.where(row >= start, end, start))
    bias[...] = jnp.where((lane >= first) & (lane <= row) & (lane < past), 0.0, -1e30)
    half = jnp.where(lane < 64, lane, lane - 64).astype(F32)
    freqs = jnp.exp(half * (-2.0 / HEAD_SIZE * math.log(rope_base)))
    angles = (row - first).astype(F32) * freqs
    cosine[...] = jnp.cos(angles)
    sine[...] = jnp.where(lane < 64, -1.0, 1.0) * jnp.sin(angles)


def weight_gather_kernel(*refs):
    (bounds, w_q, w_k, w_v, w_o, dense, norm_a, norm_m, q_gain, k_gain) = refs[:10]
    (attn_0, attn_1, dense_all, gains_all, cosine, sine, bias) = refs[10:17]
    shard, gains, send, recv, sems = refs[17:]
    place = Place()
    sib = place.sibling()
    p, z, x = place.pipe, place.at["z"], place.at["x"]
    wait_loads()
    shard[:, pl.ds(0, 1024)] = w_q[...]
    shard[:, pl.ds(1024, 128)] = w_k[...]
    shard[:, pl.ds(1152, 128)] = w_v[...]
    shard[:, pl.ds(QKV, 1024)] = w_o[...].T
    gains[...] = jnp.zeros((8, WIDTH), F32)
    gains[pl.ds(0, 1), :] = norm_a[...]
    gains[pl.ds(1, 1), :] = norm_m[...]
    gains[pl.ds(2, 1), pl.ds(0, 128)] = q_gain[...]
    gains[pl.ds(2, 1), pl.ds(128, 128)] = k_gain[...]
    greet(around(place, "xz") + [sib])

    def attn_block(attn, tile):
        def block(wanted, half):
            where = tuple(slice(None) if wanted[a] is None else wanted[a] for a in ("z", "x"))
            return attn.at[where + tile.at(half)]

        return block

    def dense_block(wanted, half):
        where = (p,) + tuple(slice(None) if wanted[a] is None else wanted[a] for a in ("z", "x"))
        rs = slice(None) if half is None else pl.ds(half * 2, 2)
        return dense_all.at[where + (rs,)]

    def run(net, order, block, first, seen):
        wanted = {axis: place.at[axis] for axis in order}
        for number, axis in enumerate(order):
            held = dict(wanted)

            def part(i, half, held=held, axis=axis):
                return block({**held, axis: i}, half)

            yield from gather_ring(
                net,
                place,
                axis,
                part,
                first if number == 0 else None,
                None if seen is None else functools.partial(seen, number, part),
            )
            wanted[axis] = None

    def dense_run(net):
        passed = [net.copy(dense, dense_all.at[p, z, x], sib), net.copy(gains, gains_all.at[p], sib)]

        def seen(number, part, i):
            passed.append(net.copy(part(i, None), part(i, None), sib))

        yield from run(net, ("x", "z"), dense_block, dense, seen)
        for made in passed:
            made.wait_recv()

    placed = [
        pltpu.make_async_copy(dense, dense_all.at[p, z, x], sems.at[0]),
        pltpu.make_async_copy(gains, gains_all.at[p], sems.at[1]),
    ]
    for made in placed:
        made.start()
    placed[0].wait()
    def rings(net, attn, seen):
        return [
            run(
                net,
                WORDERS[sub[0]],
                attn_block(attn, WTILES[sub]),
                shard.at[WTILES[sub].at()],
                None if seen is None else functools.partial(seen, i),
            )
            for i, sub in enumerate(WSUBS)
        ]

    def own_block(attn, tile):
        return attn.at[(z, x) + tile.at()]

    @pl.when(p == 0)
    def _():
        net_d = Net(send, recv)
        net_w = Net(send, recv, DENSE_COPIES)
        passing = Net(send, recv, DENSE_COPIES + RING_COPIES)
        made = pltpu.make_async_copy(shard, attn_0.at[z, x], sems.at[2])
        made.start()
        counts = [0] * len(WSUBS)

        def pass_on(sub, number, part, i):
            at = sub * 7 + 1 + counts[sub]
            counts[sub] += 1
            crossing = passing.describe(part(i, None), part(i, None), sib, at)
            crossing.start()
            passing.made.append(crossing)

        steps = rings(net_w, attn_0, pass_on)
        for step in steps:
            next(step)
        write_tables(bounds, p, cosine, sine, bias)
        for i, sub in enumerate(WSUBS):
            crossing = passing.describe(
                shard.at[WTILES[sub].at()], own_block(attn_0, WTILES[sub]), sib, i * 7
            )
            crossing.start()
            passing.made.append(crossing)
        made.wait()
        together(steps + [dense_run(net_d)])
        for net in (net_d, net_w, passing):
            net.finish()

    @pl.when(p == 1)
    def _():
        net_d = Net(send, recv)
        net_w = Net(send, recv, DENSE_COPIES)
        passing = Net(send, recv, DENSE_COPIES + RING_COPIES)
        made = pltpu.make_async_copy(shard, attn_1.at[z, x], sems.at[2])
        made.start()
        write_tables(bounds, p, cosine, sine, bias)
        together([dense_run(net_d)])

        def receive(number):
            for i, sub in enumerate(WSUBS):
                order = WORDERS[sub[0]]
                wanted = {axis: place.at[axis] for axis in order}
                if number == 0:
                    spot = own_block(attn_0, WTILES[sub])
                    passing.describe(spot, spot, sib, i * 7).wait_recv()
                else:
                    wanted[order[0]] = None
                for k, by in enumerate((-1, 1, 2)):
                    axis = order[number]
                    spot = attn_block(attn_0, WTILES[sub])(
                        {**wanted, axis: place.step(axis, by)}, None
                    )
                    passing.describe(spot, spot, sib, i * 7 + 1 + 3 * number + k).wait_recv()

        receive(0)
        made.wait()
        steps = rings(net_w, attn_1, None)
        for step in steps:
            next(step)
        receive(1)
        together(steps)
        for net in (net_d, net_w):
            net.finish()

    placed[1].wait()


def weight_gather(*args):
    attn = jax.ShapeDtypeStruct((RING, RING, ROWS, ATT), BF)
    table = jax.ShapeDtypeStruct((ROWS, 128), F32)
    return call(
        with_sem(weight_gather_kernel),
        7,
        [
            attn,
            attn,
            jax.ShapeDtypeStruct((2, RING, RING, RING, OWN, 128), F32),
            jax.ShapeDtypeStruct((2, 8, WIDTH), F32),
            table,
            table,
            table,
        ],
        [pltpu.SMEM] + [LOAD] * 9,
        [ANY] * 4 + [VM] * 3,
        [
            VM((ROWS, ATT), BF),
            VM((8, WIDTH), F32),
            pltpu.SemaphoreType.DMA((3,)),
        ],
        args,
        DENSE_COPIES + RING_COPIES + PASS_COPIES,
    )


def sum_everywhere(net, place, value, slots, pair, total):
    current = value[...]
    for number, axis in enumerate("yxz"):
        slot = slots.at[number]
        slot[place.at[axis]] = current

        def block(i, half, slot=slot):
            return slot.at[i] if half is None else slot.at[i, pl.ds(half, 1)]

        yield from gather_ring(net, place, axis, block)
        current = (slot[0] + slot[1]) + (slot[2] + slot[3])
    pair[place.pipe] = current
    crossed = net.copy(pair.at[place.pipe], pair.at[place.pipe], place.sibling())
    yield
    crossed.wait_recv()
    total[...] = pair[0] + pair[1]


TAIL_COPIES = 12 + 8 + 13 + 48
TRADES = 9
TAIL_SUBS = [
    (order[::-1], Tile(0, ROWS, lo, width, True))
    for order, lo, width in (
        (WORDERS[0], 1280, 512),
        (WORDERS[1], 1792, 512),
        (WORDERS[0], 0, 640),
        (WORDERS[1], 640, 640),
    )
]


def tail_kernel(*refs):
    refs = list(refs)
    base, dmid, gains, d_branch_0, qkv_0 = refs[:5]
    tables, gain_rows, on_core = refs[5:8], refs[8:12], refs[12:14]
    gain = gains.at[0, pl.ds(0, 1)]
    by_layer = [refs[14:19], refs[19:27]]
    given_1, stored = refs[27], refs[28:32]
    out, given_0, total = refs[32:35]
    came = refs[35:39]
    came_given, grads_out = refs[39], refs[40:42]
    part, d_qkv_v, d_gains = refs[42:45]
    both, hidden, g_all, x_all, gw_in, gw_down, turned = refs[45:52]
    attn_sems, refs = refs[52], refs[53:]
    by_layer[0].insert(1, d_qkv_v)
    by_layer[0][4:4] = [gw_in, gw_down]
    near, refs = state_bufs(refs[:8]), refs[8:]
    held, ops, part_w = refs[0], refs[1:5], refs[5]
    *bufs, slots, pair, value_v, tally, sems, send, recv = refs[6:]
    bufs = [[[bufs.pop(0) for _ in range(4)] for _ in range(2)] for sub in TAIL_SUBS]
    place = Place()
    sib = place.sibling()
    net = Net(send, recv)
    trade = Net(send, recv, TAIL_COPIES)
    mine, theirs = pl.ds(0, ROWS), pl.ds(ROWS, ROWS)
    targets = [op.at[theirs] for op in ops] + list(came)

    def owed(layer, which):
        return [
            trade.describe(by_layer[layer][i], targets[i], sib, i) for i in which
        ]

    w_out, w_qkv = g_all.at[EVERY + (pl.ds(0, 1024),)], x_all.at[EVERY + (pl.ds(0, QKV),)]
    fetched_w = fetch_attention(on_core, [(QKV, w_out), (0, w_qkv)], attn_sems)

    def exchange(which):
        for core in range(2):

            @pl.when(place.pipe == core)
            def _(core=core):
                for i in which:
                    pltpu.make_async_copy(by_layer[core][i], ops[i].at[mine], sems.at[i]).start()
                for made in owed(1 - core, which):
                    made.start()

    greet(around(place, "xyz") + [sib])
    exchange((2, 3))
    attention_backward(
        0,
        d_branch_0,
        qkv_0,
        fetched_w,
        w_out,
        w_qkv,
        gains,
        tables,
        part,
        d_qkv_v,
        d_gains,
    )
    exchange((0, 1))
    loads = [
        pltpu.make_async_copy(src, dst, attn_sems.at[2 + i])
        for i, (src, dst) in enumerate(zip(stored, (both, hidden, g_all, x_all)))
    ]
    for made in loads:
        made.start()
    value_v[...] = jnp.zeros((2, GAIN_ROWS, 128), F32)
    for layer, row, source in ((0, 16, 0), (1, 0, 1), (1, 16, 2)):
        for i in range(16):
            value_v[layer, pl.ds(row + i, 1), :] = gain_rows[source][:, pl.ds(i * 128, 128)]
    value_v[0, pl.ds(32, 8), :] = d_gains[...]
    value_v[1, pl.ds(32, 8), :] = gain_rows[3][...]
    tally[...] = jnp.zeros((1, WIDTH), F32)

    def state_run():
        def put(t, rs, rows):
            held[t, rs, :] = rows

        yield from in_turn([reduce_tensor(net, place, stream, part, near) for stream in range(2)])
        for stream in range(2):
            state_back(place, stream, base, dmid, gain, near, tally, put)
        for i in range(16):
            value_v[0, pl.ds(i, 1), :] = tally[:, pl.ds(i * 128, 128)]
        yield from in_turn([gather_tensor(net, place, stream, held) for stream in range(2)])

        @pl.when(place.pipe == 1)
        def _():
            trade.describe(held, came_given, sib, 8).start()

        yield from sum_everywhere(net, place, value_v, slots, pair, total)

    state_step = state_run()
    next(state_step)
    steps = []

    def start_reduce(which):
        for sub in which:
            order, tile = TAIL_SUBS[sub]

            def source(wanted, half, tile=tile):
                where = tuple(wanted.get(a, slice(None)) for a in ("z", "x"))
                return part_w.at[where + tile.at(half)]

            step = reduce_all(net, place, order, ("z", "x"), source, tile, bufs[sub])
            next(step)
            steps.append(step)

    for left, right, lo, width, subs in ((3, 2, QKV, 1024, (0, 1)), (0, 1, 0, QKV, (2, 3))):
        for i in (left, right):
            pltpu.make_async_copy(by_layer[0][i], ops[i].at[mine], sems.at[i]).wait()
            trade.describe(ops[i].at[theirs], targets[i], sib, i).wait_recv()

        def product(i, _, left=left, right=right, lo=lo, width=width):
            dims = pl.ds(pl.multiple_of(i * 512, 512), 512)
            made = dot_tn(ops[left][:, dims], ops[right][...]).astype(BF)
            part_w[i, :, :, pl.ds(lo, width)] = made.reshape(RING, ROWS, width)
            return 0

        lax.fori_loop(0, RING, product, 0)
        start_reduce(subs)
    for core in range(2):

        @pl.when(place.pipe == core)
        def _(core=core):
            for made in owed(1 - core, (6, 7)):
                made.start()
            if core == 0:
                trade.describe(given_1, came_given, sib, 8).start()

    for made in loads:
        made.wait()
    fill = weight_grads(
        ((hidden, 0, g_all, gw_down), (both, 0, x_all, gw_in), (both, HIDDEN, x_all, gw_in)), turned
    )
    for number in range(6):
        next(fill)
        if number % 2:
            next(state_step)
    for step in steps:
        next(step)
    for number in range(6):
        next(fill)
        if number % 2:
            next(state_step)
    stores = [
        pltpu.make_async_copy(src, dst, attn_sems.at[i])
        for i, (src, dst) in enumerate(zip((gw_in, gw_down), grads_out))
    ]
    for made in stores:
        made.start()
    for core in range(2):

        @pl.when(place.pipe == core)
        def _(core=core):
            for made in owed(1 - core, (4, 5)):
                made.start()

    together([state_step] + steps)
    for (_, tile), buf in zip(TAIL_SUBS, bufs):
        out[tile.at()] = buf[-1][2][...].astype(F32)
    given_0[...] = held[...]
    net.finish()
    for core in range(2):

        @pl.when(place.pipe == core)
        def _(core=core):
            for made in owed(1 - core, range(8)):
                made.wait_send()
            source = given_1 if core == 0 else held
            trade.describe(source, came_given, sib, 8).wait_send()

    for made in stores:
        made.wait()
    for i in range(4, 8):
        trade.describe(targets[i], targets[i], sib, i).wait_recv()
    trade.describe(came_given, came_given, sib, 8).wait_recv()


def tail(base, dmid, gains, d_branch, qkv, tables, gain_rows, on_core, by_layer, given_1, stored):
    shapes = [x.shape for x in by_layer[1]]
    return call(
        tail_kernel,
        8,
        [
            jax.ShapeDtypeStruct((ROWS, ATT), F32),
            jax.ShapeDtypeStruct((RING, OWN, WIDTH), BF),
            jax.ShapeDtypeStruct((2, GAIN_ROWS, 128), F32),
        ]
        + [jax.ShapeDtypeStruct(shape, BF) for shape in shapes[4:]]
        + [jax.ShapeDtypeStruct((RING, OWN, WIDTH), BF)]
        + [jax.ShapeDtypeStruct((768, WIDTH), BF), jax.ShapeDtypeStruct((HIDDEN, WIDTH), BF)],
        [Load((RING, OWN, WIDTH), of_pipe)] + [LOAD] * 11 + [ANY] * 20,
        [VM] * 3 + [ANY] * 7,
        [
            VM((RING, OWN, WIDTH), BF),
            VM((ROWS, QKV), BF),
            VM((8, 128), F32),
            VM((RING, RING, RING, OWN, 768), BF),
            VM((RING, RING, RING, OWN, HIDDEN), BF),
            VM(TOKENS_ALL, BF),
            VM(TOKENS_ALL, BF),
            VM((768, WIDTH), BF),
            VM((HIDDEN, WIDTH), BF),
            VM((HIDDEN, 2048), BF),
            pltpu.SemaphoreType.DMA((6,)),
        ]
        + state_scratch()
        + [VM((RING, OWN, WIDTH), BF)]
        + [VM((2 * ROWS, shape[1]), BF) for shape in shapes[:4]]
        + [VM((RING, RING, ROWS, ATT), BF)]
        + flat([reduce_scratch(2, tile) for _, tile in TAIL_SUBS])
        + [
            VM((3, RING, 2, GAIN_ROWS, 128), F32),
            VM((2, 2, GAIN_ROWS, 128), F32),
            VM((2, GAIN_ROWS, 128), F32),
            VM((1, WIDTH), F32),
            pltpu.SemaphoreType.DMA((4,)),
        ],
        (
            base.reshape(2, RING, OWN, WIDTH),
            dmid,
            gains,
            d_branch,
            qkv,
            *tables,
            *gain_rows,
            *on_core,
            *by_layer[0],
            *by_layer[1],
            given_1,
            *stored,
        ),
        TAIL_COPIES + TRADES,
    )


def write_kernel(*refs):
    refs = list(refs)
    attn, total = refs[:2]
    in_0, in_1, in_came, down_0, down_1, down_came = refs[2:8]
    act_0, act_1, act_came, given_0, given_1, given_came = refs[8:14]
    d_gate, d_up, d_down, acts, givens, d_query, d_key, d_value, d_out = refs[14:23]
    d_norm_a, d_norm_m, d_q, d_k = refs[23:27]
    pieces, pieces_came, sums, rows, rows_f, sem_in, sem_out = refs[27:]
    pipe = lax.axis_index("pipe")
    adds = []

    def load(i):
        which, lo = divmod(i * 192, HIDDEN)
        own = (in_0, in_1) if which < 2 else (down_0, down_1)
        came = in_came if which < 2 else down_came
        rs = pl.ds(lo + (HIDDEN if which == 1 else 0), 192)
        for core in range(2):

            @pl.when(pipe == core)
            def _(source=own[core]):
                pltpu.make_async_copy(source.at[rs], pieces.at[i], sem_in.at[2 * i]).start()

        pltpu.make_async_copy(came.at[rs], pieces_came.at[i], sem_in.at[2 * i + 1]).start()
        adds.append((d_gate, d_up, d_down)[which].at[pl.ds(lo, 192)])

    sources = ((act_0, act_1), (given_0, given_1))

    def load_rows(k):
        for core in range(2):

            @pl.when(pipe == core)
            def _(source=sources[k][core]):
                pltpu.make_async_copy(source, rows.at[2 * k], sem_in.at[12 + 2 * k]).start()

        came = (act_came, given_came)[k]
        pltpu.make_async_copy(came, rows.at[2 * k + 1], sem_in.at[13 + 2 * k]).start()

    for i in range(3):
        load(i)
    stores = []
    wait_loads()
    for i in range(16):
        d_norm_a[:, pl.ds(i * 128, 128)] = total[pipe, pl.ds(i, 1), :]
        d_norm_m[:, pl.ds(i * 128, 128)] = total[pipe, pl.ds(16 + i, 1), :]
    d_q[...] = total[pipe, pl.ds(32, 1), :]
    d_k[...] = total[pipe, pl.ds(33, 1), :]
    d_query[...] = attn[:, pl.ds(0, 1024)]
    d_key[...] = attn[:, pl.ds(1024, 128)]
    d_value[...] = attn[:, pl.ds(1152, 128)]
    d_out[...] = attn[:, pl.ds(QKV, 1024)].T
    for i in range(6):
        pltpu.make_async_copy(in_0.at[pl.ds(0, 192)], pieces.at[i], sem_in.at[2 * i]).wait()
        pltpu.make_async_copy(in_0.at[pl.ds(0, 192)], pieces_came.at[i], sem_in.at[2 * i + 1]).wait()
        if i < 3:
            load(i + 3)
        elif i < 5:
            load_rows(i - 3)

        def each(j, _, i=i):
            rs = pl.ds(pl.multiple_of(j * 32, 32), 32)
            sums[i, rs, :] = pieces[i, rs, :].astype(F32) + pieces_came[i, rs, :].astype(F32)
            return 0

        lax.fori_loop(0, 6, each, 0)
        made = pltpu.make_async_copy(sums.at[i], adds[i], sem_out.at[i])
        made.start()
        stores.append(made)
    for k, out in enumerate((acts, givens)):
        for n in range(2):
            i = 2 * k + n
            pltpu.make_async_copy(act_0, rows.at[i], sem_in.at[12 + i]).wait()

            def each(j, _, i=i):
                rs = pl.ds(pl.multiple_of(j * 16, 16), 16)
                rows_f[i, rs, :] = rows[i, rs, :].astype(F32)
                return 0

            lax.fori_loop(0, 8, each, 0)
            spot = out.at[pipe if n == 0 else 1 - pipe]
            made = pltpu.make_async_copy(rows_f.at[i], spot, sem_out.at[6 + i])
            made.start()
            stores.append(made)
    for made in stores:
        made.wait()


def write_outputs(*args):
    kernel, held, kinds = loading(write_kernel, [LOAD] * 2 + [ANY] * 12, args)
    return pl.pallas_call(
        kernel,
        out_shape=[jax.ShapeDtypeStruct((HIDDEN, WIDTH), F32)] * 3
        + [jax.ShapeDtypeStruct((2, ROWS, WIDTH), F32)] * 2
        + [
            jax.ShapeDtypeStruct((ROWS, 1024), F32),
            jax.ShapeDtypeStruct((ROWS, 128), F32),
            jax.ShapeDtypeStruct((ROWS, 128), F32),
            jax.ShapeDtypeStruct((1024, ROWS), F32),
            jax.ShapeDtypeStruct((1, WIDTH), F32),
            jax.ShapeDtypeStruct((1, WIDTH), F32),
            jax.ShapeDtypeStruct((1, 128), F32),
            jax.ShapeDtypeStruct((1, 128), F32),
        ],
        in_specs=[pl.BlockSpec(memory_space=kind) for kind in kinds],
        out_specs=[pl.BlockSpec(memory_space=ANY)] * 5 + [pl.BlockSpec(memory_space=VM)] * 8,
        scratch_shapes=[
            VM((6, 192, WIDTH), BF),
            VM((6, 192, WIDTH), BF),
            VM((6, 192, WIDTH), F32),
            VM((4, ROWS, WIDTH), BF),
            VM((4, ROWS, WIDTH), F32),
            pltpu.SemaphoreType.DMA((16,)),
            pltpu.SemaphoreType.DMA((10,)),
        ]
        + held,
        compiler_params=pltpu.CompilerParams(vmem_limit_bytes=60 * 2**20),
        cost_estimate=pl.CostEstimate(flops=0, bytes_accessed=24 * 2**20, transcendentals=0),
    )(*args)


def dot_nn(a, b):
    return lax.dot_general(a, b, (((1,), (0,)), ((), ())), preferred_element_type=F32)


def dot_nt(a, b):
    return lax.dot_general(a, b, (((1,), (1,)), ((), ())), preferred_element_type=F32)


def dot_tn(a, b):
    return lax.dot_general(a, b, (((0,), (0,)), ((), ())), preferred_element_type=F32)


def stack_heads(values, count):
    return jnp.concatenate([values[:, h * 128 : (h + 1) * 128] for h in range(count)], axis=0)


def unstack_heads(values, count):
    return jnp.concatenate([values[h * ROWS : (h + 1) * ROWS, :] for h in range(count)], axis=1)


def turn(values, cosine, sine):
    return values * cosine + pltpu.roll(values, 64, 1) * sine


def over_heads(table):
    return jnp.concatenate([table] * 8, axis=0)


SCORE_SCALE = HEAD_SIZE ** (-0.5)


def fetch_attention(sources, parts, sem):
    made = []
    for number, (lo, spot) in enumerate(parts):
        cs = pl.ds(lo, spot.shape[-1])
        for core, source in enumerate(sources):

            @pl.when(lax.axis_index("pipe") == core)
            def _(source=source):
                source = source.at[EVERY + (cs,)]
                pltpu.make_async_copy(source, spot, sem.at[number]).start()

        made.append(pltpu.make_async_copy(sources[0].at[EVERY + (cs,)], spot, sem.at[number]))
    return made


EVERY = (slice(None),) * 4


def columns(spot):
    return spot[...].reshape(WIDTH, spot.shape[-1])


def head_gains(gains, layer):
    row = pl.ds(2, 1)
    return gains[layer, row, pl.ds(0, 128)], gains[layer, row, pl.ds(128, 128)]


def attention_forward(layer, state, fetched, parts, gains, tables, branch, normed, qkv, attended):
    q_gain, k_gain = head_gains(gains, layer)
    cos, sin, bias = (table[...] for table in tables)
    rows = state[...].reshape(ROWS, WIDTH).astype(F32)
    normed[...] = (rows * inv_rms(rows) * gains[layer, pl.ds(0, 1), :]).astype(BF)
    fetched[0].wait()
    qkv[...] = dot_nn(normed[...], columns(parts[0][1]))
    query = stack_heads(qkv[:, pl.ds(0, 1024)], 8)
    key = qkv[:, pl.ds(1024, 128)]
    value = qkv[:, pl.ds(1152, 128)].astype(BF)
    q_rot = turn(query * inv_rms(query) * q_gain, over_heads(cos), over_heads(sin)).astype(BF)
    k_rot = turn(key * inv_rms(key) * k_gain, cos, sin).astype(BF)
    scores = dot_nt(q_rot, k_rot) * SCORE_SCALE + over_heads(bias)
    grown = jnp.exp(scores - jnp.max(scores, axis=-1, keepdims=True))
    probs = (grown / jnp.sum(grown, axis=-1, keepdims=True)).astype(BF)
    attended[...] = unstack_heads(dot_nn(probs, value), 8).astype(BF)
    total = None
    for made, (lo, spot) in zip(fetched[1:], parts[1:]):
        made.wait()
        heads = attended[:, pl.ds(lo - QKV, spot.shape[-1])]
        term = dot_nt(heads, columns(spot))
        total = term if total is None else total + term
    branch[...] = total.astype(BF).reshape(RING, OWN, WIDTH)


def attention_backward(layer, d_branch, qkv, fetched, w_out, w_qkv, gains, tables, d_normed, d_qkv, d_gains):
    q_gain, k_gain = head_gains(gains, layer)
    cos, sin, bias = (table[...] for table in tables)
    cos8, sin8 = over_heads(cos), over_heads(sin)
    query = stack_heads(qkv[:, pl.ds(0, 1024)], 8)
    key = qkv[:, pl.ds(1024, 128)]
    value = qkv[:, pl.ds(1152, 128)].astype(BF)
    q_rot = turn(query * inv_rms(query) * q_gain, cos8, sin8).astype(BF)
    k_rot = turn(key * inv_rms(key) * k_gain, cos, sin).astype(BF)
    scores = dot_nt(q_rot, k_rot) * SCORE_SCALE + over_heads(bias)
    grown = jnp.exp(scores - jnp.max(scores, axis=-1, keepdims=True))
    prob = grown / jnp.sum(grown, axis=-1, keepdims=True)
    fetched[0].wait()
    d_att = dot_nn(d_branch[...].reshape(ROWS, WIDTH), columns(w_out)).astype(BF)
    d_att = stack_heads(d_att, 8)
    d_prob = dot_nt(d_att, value)
    d_value = dot_tn(prob.astype(BF), d_att)
    delta = jnp.sum(prob * d_prob, axis=-1, keepdims=True)
    d_scores = (prob * (d_prob - delta)).astype(BF)
    d_q_rot = dot_nn(d_scores, k_rot) * SCORE_SCALE
    d_k_rot = dot_tn(d_scores, q_rot) * SCORE_SCALE
    d_query, q_rows = norm_back(turn(d_q_rot, cos8, -sin8), query, q_gain)
    d_key, k_rows = norm_back(turn(d_k_rot, cos, -sin), key, k_gain)
    d_qkv[:, pl.ds(0, 1024)] = unstack_heads(d_query, 8).astype(BF)
    d_qkv[:, pl.ds(1024, 128)] = d_key.astype(BF)
    d_qkv[:, pl.ds(1152, 128)] = d_value.astype(BF)
    fetched[1].wait()
    made = dot_nt(d_qkv[...], columns(w_qkv))
    d_normed[...] = made.astype(BF).reshape(RING, OWN, WIDTH)
    d_gains[...] = jnp.zeros((8, 128), F32)
    d_gains[pl.ds(0, 1), :] = jnp.sum(q_rows, axis=0, keepdims=True)
    d_gains[pl.ds(1, 1), :] = jnp.sum(k_rows, axis=0, keepdims=True)


def plane_at(chunk, i):
    last = ORDERS[chunk][-1]
    return tuple(i if axis == last else slice(None) for axis in ("z", "x", "y"))


def fetch_experts(place, layer, own, other, dst, sems):
    spots = [dst[0].at[pl.ds(0, 2)], dst[0].at[pl.ds(2, 2)], dst[1]]
    for refs, mine in ((own, True), (other, False)):
        here = place.pipe == layer if mine else place.pipe != layer

        @pl.when(here)
        def _(refs=refs):
            for i, (ref, spot) in enumerate(zip(refs, spots)):
                pltpu.make_async_copy(ref, spot, sems.at[i]).start()

    return [
        pltpu.make_async_copy(ref, spot, sems.at[i]) for i, (ref, spot) in enumerate(zip(own, spots))
    ]


F, T = "f", "t"
FORWARD = (0, 1) * 5 + (
    *(0, 0, 0, 1, 0, 0, 0, 0, 0, 0, 1, 1, 0, 1, 1, 0, 1, 1, 1),
    *(0, 1, 0, 1, 0, 1, 0, 0, 1, 0, 1, 0, 1, 1, 1, 1, 1),
)
BACKWARD_0 = (
    *(0, 1, 0, 1, 0, 0, 1, 1, 0, 0, 0, 0, 1, 0, 1, 1, 0, 0, 0, 0),
    *(1, 1, 1, 0, 0, 1, 1, 1, F, F, 0, F, 1, F, T, F, 0, 1, 0, F),
    *(1, T, F, F, 0, F, 1, F, 0, T, F, 1, 0, T, 1, T, 1, 0, T, 1),
    *(T, 0, F, T, 1, T, 1),
)
BACKWARD_1 = (
    *(0, 0, 0, 1, 1, 0, 1, 1, 0, 0, 0, 0, 0, 1, 0, 1, 0, 0, 0, 0),
    *(1, 1, 1, 1, 0, 0, 1, 1, 1, 1, F, T, F, 0, 1, T, F, 0, F, F),
    *(1, 0, F, 0, 1, 0, T, 1, F, F, 1, F, T, 1, F, 0, T, 1, T, F),
    *(T, 1, T, F, 1, 0, T),
)


def pick_weight(place, rows, lane):
    first = EXPERTS * place.pipe + 2 * (place.at["z"] * RING + place.at["x"])
    column = lax.broadcasted_iota(jnp.int32, rows.shape, 2)
    low = jnp.sum(jnp.where(column == first, rows, 0.0), axis=2, keepdims=True)
    high = jnp.sum(jnp.where(column == first + 1, rows, 0.0), axis=2, keepdims=True)
    return jnp.where(lane < 192, low, high)


def stream_steps(net, place, stream, spread_rows, own, gathered, compute, mix, part, bufs, make, finish, held):
    yield from spread_rows(stream)
    gather = gather_tokens(net, place, stream, own, gathered)
    for _ in range(5):
        next(gather)
        yield
    for chunk in range(3):
        compute(chunk, stream, 0)
    yield
    next(gather)
    yield
    for by in (-1, 1):
        for chunk in range(3):
            compute(chunk, stream, by)
        yield
    together([gather])
    yield
    for chunk in range(3):
        compute(chunk, stream, 2)
    yield
    mix(stream)
    yield
    yield from reduce_tokens(net, place, stream, part, bufs, make)
    finish(stream)
    yield from gather_tensor(net, place, stream, held)


def layer_forward_kernel(layer, *refs):
    refs = list(refs)
    (base, gains, dense), tables, on_core, refs = refs[:3], refs[3:6], refs[6:8], refs[4:]
    gain = gains.at[layer, pl.ds(1, 1)]
    own_w, other_w = refs[4:7], refs[7:10]
    refs = refs[10:]
    if layer == 0:
        attn_1, refs = refs[0], refs[1:]
    out, middle, kept, state = refs[:4]
    results, refs = refs[4:7], refs[7:]
    if layer == 0:
        attn_came, refs = refs[0], refs[1:]
    part, *attn_v, rest_w, attn_sems = refs[:6]
    refs = refs[6:]
    near, refs = state_bufs(refs[:8]), refs[8:]
    (own, held, x_all, part_all, acc, kept_v, hidden, w_in, w_down, spread) = refs[:10]
    *bufs, sems, send, recv = refs[10:]
    bufs = token_bufs(bufs)
    place = Place()
    net = Net(send, recv)
    fetched = fetch_experts(place, layer, own_w, other_w, (w_in, w_down), sems)
    fetched.append(pltpu.make_async_copy(dense.at[layer], spread, sems.at[5]))
    fetched[-1].start()
    parts = [
        (0, part_all.at[EVERY + (pl.ds(0, QKV),)]),
        (QKV, part_all.at[EVERY + (pl.ds(QKV, WIDTH - QKV),)]),
        (WIDTH, rest_w),
    ]
    fetched_w = fetch_attention(on_core, parts, attn_sems)

    def attend():
        attention_forward(layer, base, fetched_w, parts, gains, tables, part, *attn_v)

    if layer == 0:
        crossing = net.describe(attn_1, attn_came, place.sibling(), FORWARD_COPIES)
        greet_sibling(place, around(place, "xyz"), attend)

        @pl.when(place.pipe == 1)
        def _():
            crossing.start()

    else:
        greet(around(place, "xyz"), attend)
    attn_saved = [
        pltpu.make_async_copy(src, dst, attn_sems.at[3 + i])
        for i, (src, dst) in enumerate(zip(attn_v, results))
    ]
    for made in attn_saved:
        made.start()
    z, x, t = place.at["z"], place.at["x"], place.at["y"]

    def clear(i, _):
        acc[lax.div(i, 16), lax.rem(lax.div(i, 4), 4), lax.rem(i, 4)] = jnp.zeros((OWN, 768), F32)
        return 0

    def spread_rows(stream):
        yield from reduce_tensor(net, place, stream, part, near)
        rs = pl.ds(stream * 16, 16)
        value = base[t, rs, :].astype(F32) + near[stream][2][...].astype(F32)
        middle[rs, :] = value
        rounded = (value * inv_rms(value) * gain[...]).astype(BF)
        own[rs, :] = rounded
        x_all[z, x, t, rs, :] = rounded

    def gate_up(chunk, stream, by):
        rs, cs = TILES[chunk, stream].at()
        at = plane_at(chunk, place.step(ORDERS[chunk][-1], by)) + (rs,)
        rows = x_all[at + (cs,)].reshape(256, cs.size)
        made = dot_nt(rows, w_in[:, :, cs].reshape(768, cs.size))
        acc[at] = acc[at] + made.reshape(RING, RING, 16, 768)

    lane = lax.broadcasted_iota(jnp.int32, (RING, 16, HIDDEN), 2)
    saved = [
        pltpu.make_async_copy(x_all, out, sems.at[3]),
        pltpu.make_async_copy(kept_v, kept, sems.at[4]),
    ]

    mixed = []

    def mix(stream):
        def tile(i, _):
            at = (lax.div(i, 4), lax.rem(i, 4), slice(None), pl.ds(stream * 16, 16))
            both = acc[at]
            kept_v[at] = both.astype(BF)
            gate, up = both[:, :, :HIDDEN], both[:, :, HIDDEN:]
            weight = pick_weight(place, spread[at], lane)
            hidden[at] = (gate * jax.nn.sigmoid(gate) * up * weight).astype(BF)
            return 0

        lax.fori_loop(0, 16, tile, 0)
        mixed.append(stream)
        if len(mixed) == 2:
            for made in saved:
                made.start()

    def down(chunk, stream, by):
        rs, cs = TILES[chunk, stream].at()
        at = plane_at(chunk, place.step(ORDERS[chunk][-1], by)) + (rs,)
        made = dot_nn(hidden[at].reshape(256, HIDDEN), w_down[:, :, cs].reshape(HIDDEN, cs.size))
        part_all[at + (cs,)] = made.astype(BF).reshape(RING, RING, 16, cs.size)

    def finish(stream):
        rs = pl.ds(stream * 16, 16)
        held[t, rs, :] = (middle[rs, :] + token_sums(bufs, stream)).astype(BF)

    steps = {
        i: stream_steps(
            net, place, i, spread_rows, own, x_all, gate_up, mix, part_all, bufs, down, finish, held
        )
        for i in range(2)
    }
    for i in range(2):
        next(steps[i])
    lax.fori_loop(0, 64, clear, 0)
    for made in fetched:
        made.wait()
    run_schedule(FORWARD, steps)
    net.finish()
    state[...] = held[...]
    for made in saved + attn_saved:
        made.wait()
    if layer == 0:

        @pl.when(place.pipe == 0)
        def _():
            crossing.wait_recv()

        @pl.when(place.pipe == 1)
        def _():
            crossing.wait_send()


FORWARD_COPIES = 12 + GATHER_COPIES + REDUCE_COPIES + 8


def layer_forward(layer, base, gains, dense, tables, on_core, own_w, other_w, *attn_1):
    outs = [
        jax.ShapeDtypeStruct(TOKENS_ALL, BF),
        jax.ShapeDtypeStruct((OWN, WIDTH), F32),
        jax.ShapeDtypeStruct((RING, RING, RING, OWN, 768), BF),
        jax.ShapeDtypeStruct((RING, OWN, WIDTH), BF),
        jax.ShapeDtypeStruct((ROWS, WIDTH), BF),
        jax.ShapeDtypeStruct((ROWS, QKV), F32),
        jax.ShapeDtypeStruct((ROWS, 1024), BF),
    ]
    kinds = [ANY, VM, ANY, VM, ANY, ANY, ANY]
    if layer == 0:
        outs.append(jax.ShapeDtypeStruct((RING, RING, ROWS, ATT), BF))
        kinds.append(ANY)
    return call(
        functools.partial(layer_forward_kernel, layer),
        1 + 20 * layer,
        outs,
        [Load((RING, OWN, WIDTH), of_pipe if layer == 0 else None), LOAD, ANY, LOAD, LOAD, LOAD]
        + [ANY] * (8 + len(attn_1)),
        kinds,
        [
            VM((RING, OWN, WIDTH), BF),
            VM((ROWS, WIDTH), BF),
            VM((ROWS, QKV), F32),
            VM((ROWS, 1024), BF),
            VM((RING, RING, RING, OWN, ATT - WIDTH), BF),
            pltpu.SemaphoreType.DMA((6,)),
        ]
        + state_scratch()
        + [
            VM((OWN, WIDTH), BF),
            VM((RING, OWN, WIDTH), BF),
            VM(TOKENS_ALL, BF),
            VM(TOKENS_ALL, BF),
            VM((RING, RING, RING, OWN, 768), F32),
            VM((RING, RING, RING, OWN, 768), BF),
            VM((RING, RING, RING, OWN, HIDDEN), BF),
            VM((4, 192, WIDTH), BF),
            VM((2, 192, WIDTH), BF),
            VM((RING, RING, RING, OWN, 128), F32),
        ]
        + token_scratch()
        + [pltpu.SemaphoreType.DMA((6,))],
        (
            base.reshape(*base.shape[:-2], RING, OWN, WIDTH),
            gains,
            dense,
            *tables,
            *on_core,
            *own_w,
            *other_w,
            *attn_1,
        ),
        FORWARD_COPIES + 1,
        60,
    )


def weight_grads(groups, turned):
    for left, lo, right, out in groups:
        turned[...] = left[EVERY + (pl.ds(lo, HIDDEN),)].reshape(2048, HIDDEN).T
        for j in range(4):
            cs = pl.ds(j * 512, 512)
            made = dot_nn(turned[...], right[EVERY + (cs,)].reshape(2048, 512))
            out[pl.ds(lo, HIDDEN), cs] = made.astype(BF)
            yield


def layer_backward_kernel(layer, *refs):
    refs = list(refs)
    if layer == 1:
        given, refs = refs[0], refs[1:]
    else:
        (base, dmid_next, d_branch_next, qkv_next), refs = refs[:4], refs[4:]
        tables, on_core, refs = refs[:3], refs[3:5], refs[5:]
    (middle, gains, dense, kept, tokens) = refs[:5]
    gain, gain_next = gains.at[layer, pl.ds(1, 1)], gains.at[1, pl.ds(0, 1)]
    own_w, other_w = refs[5:8], refs[8:11]
    dmid, d_branch, tally, d_gain = refs[11:15]
    refs = refs[15:]
    if layer == 1:
        (grad_in, grad_down), refs = refs[:2], refs[2:]
    else:
        operands_out, refs = refs[:3], refs[3:]
    if layer == 0:
        (given_out, d_gain_next, d_qkv_out, d_gains_next), refs = refs[:4], refs[4:]
        (part, d_qkv_v, attn_sems), refs = refs[:3], refs[3:]
        near, refs = state_bufs(refs[:8]), refs[8:]
    (own, held, held_d, g_all, x_all, part_all, part_d, acc, both, hidden, w_in, w_down) = refs[:12]
    spread, refs = refs[12], refs[13:]
    if layer == 1:
        (gw_in, gw_down, turned), refs = refs[:3], refs[3:]
    *bufs, sems, send, recv = refs
    tally_bufs = [[bufs.pop(0) for _ in range(4)] for _ in range(3)]
    bufs = token_bufs(bufs)
    place = Place()
    net = Net(send, recv)
    z, x, t = place.at["z"], place.at["x"], place.at["y"]
    fetched = fetch_experts(place, layer, own_w, other_w, (w_in, w_down), sems)
    d_gain[...] = jnp.zeros((1, WIDTH), F32)
    if layer == 0:
        d_gain_next[...] = jnp.zeros((1, WIDTH), F32)
    mixed = []
    for src, dst, i in ((kept, both, 3), (dense.at[layer], spread, 7)):
        made = pltpu.make_async_copy(src, dst, sems.at[i])
        made.start()
        fetched.append(made)
    attend = None
    if layer == 0:
        w_out = part_all.at[EVERY + (pl.ds(0, 1024),)]
        w_qkv = x_all.at[EVERY + (pl.ds(0, QKV),)]
        fetched_w = fetch_attention(on_core, [(QKV, w_out), (0, w_qkv)], attn_sems)

        def attend():
            attention_backward(
                1,
                d_branch_next,
                qkv_next,
                fetched_w,
                w_out,
                w_qkv,
                gains,
                tables,
                part,
                d_qkv_v,
                d_gains_next,
            )

    greet(around(place, "xyz"), attend)
    if layer == 1:
        token_copy = pltpu.make_async_copy(tokens, x_all, sems.at[4])
        token_copy.start()
    else:
        saving = pltpu.make_async_copy(d_qkv_v, d_qkv_out, attn_sems.at[2])
        saving.start()
        stores = [
            pltpu.make_async_copy(src, dst, sems.at[4 + i])
            for i, (src, dst) in enumerate(zip((both, hidden, g_all), operands_out))
        ]

    def clear(i, _):
        acc[lax.div(i, 16), lax.rem(lax.div(i, 4), 4), lax.rem(i, 4)] = jnp.zeros((OWN, HIDDEN), F32)
        return 0

    def spread_rows(stream):
        rs = pl.ds(stream * 16, 16)
        if layer == 0:

            def put(t, rs, value):
                own[rs, :] = value

            yield from reduce_tensor(net, place, stream, part, near)
            state_back(place, stream, base, dmid_next, gain_next, near, d_gain_next, put)
        else:
            own[rs, :] = given[t, rs, :]
            yield
            yield
        g_all[z, x, t, rs, :] = own[rs, :]

    def back_hidden(chunk, stream, by):
        rs, cs = TILES[chunk, stream].at()
        at = plane_at(chunk, place.step(ORDERS[chunk][-1], by)) + (rs,)
        rows = g_all[at + (cs,)].reshape(256, cs.size)
        made = dot_nt(rows, w_down[:, :, cs].reshape(HIDDEN, cs.size))
        acc[at] = acc[at] + made.reshape(RING, RING, 16, HIDDEN)

    lane = lax.broadcasted_iota(jnp.int32, (RING, 16, HIDDEN), 2)
    column = lax.broadcasted_iota(jnp.int32, (RING, 16, 128), 2)
    expert = 2 * (z * RING + x)

    def mix(stream):
        def tile(i, _):
            at = (lax.div(i, 4), lax.rem(i, 4), slice(None), pl.ds(stream * 16, 16))
            gate = both[at + (pl.ds(0, HIDDEN),)].astype(F32)
            up = both[at + (pl.ds(HIDDEN, HIDDEN),)].astype(F32)
            d_hidden = acc[at]
            sig = jax.nn.sigmoid(gate)
            silu = gate * sig
            value = silu * up
            dots = value * d_hidden
            low = jnp.sum(jnp.where(lane < 192, dots, 0.0), axis=2, keepdims=True)
            high = jnp.sum(jnp.where(lane < 192, 0.0, dots), axis=2, keepdims=True)
            part_d[at] = (
                jnp.where(column == expert, low, 0.0) + jnp.where(column == expert + 1, high, 0.0)
            ).astype(BF)
            weight = pick_weight(place, spread[at], lane)
            d_hidden = d_hidden * weight
            hidden[at] = (value * weight).astype(BF)
            d_gate = d_hidden * up * sig * (1.0 + gate * (1.0 - sig))
            both[at + (pl.ds(0, HIDDEN),)] = d_gate.astype(BF)
            both[at + (pl.ds(HIDDEN, HIDDEN),)] = (d_hidden * silu).astype(BF)
            return 0

        lax.fori_loop(0, 16, tile, 0)
        mixed.append(stream)
        if layer == 0 and len(mixed) == 2:
            given_out[...] = g_all[z, x]
            for made in stores:
                made.start()

    def back_rows(chunk, stream, by):
        rs, cs = TILES[chunk, stream].at()
        at = plane_at(chunk, place.step(ORDERS[chunk][-1], by)) + (rs,)
        made = dot_nn(both[at].reshape(256, 768), w_in[:, :, cs].reshape(768, cs.size))
        part_all[at + (cs,)] = made.astype(BF).reshape(RING, RING, 16, cs.size)

    def tallying():
        yield from reduce_all(
            net,
            place,
            ("x", "z", "y"),
            ("z", "x", "y"),
            token_block(part_d, TALLY_TILE),
            TALLY_TILE,
            tally_bufs,
        )
        held_d[t, :, :] = tally_bufs[-1][2][...]
        yield from gather_ring(net, place, "y", tensor_blocks(held_d, TALLY_TILE))

    def finish(stream):
        rs = pl.ds(stream * 16, 16)
        back, rows = norm_back(token_sums(bufs, stream), middle[rs, :], gain[...])
        value = own[rs, :].astype(F32) + back
        dmid[rs, :] = value
        held[t, rs, :] = value.astype(BF)
        add_rows(d_gain, rows)

    steps = {
        i: stream_steps(
            net,
            place,
            i,
            spread_rows,
            own,
            g_all,
            back_hidden,
            mix,
            part_all,
            bufs,
            back_rows,
            finish,
            held,
        )
        for i in range(2)
    }
    for i in range(2):
        next(steps[i])
    lax.fori_loop(0, 64, clear, 0)
    for made in fetched:
        made.wait()
    steps[T] = tallying()
    if layer == 1:

        def fill():
            token_copy.wait()
            yield from weight_grads(
                (
                    (hidden, 0, g_all, gw_down),
                    (both, 0, x_all, gw_in),
                    (both, HIDDEN, x_all, gw_in),
                ),
                turned,
            )

        steps[F] = fill()
        run_schedule(BACKWARD_1, steps)
        stores = []
        for src, dst, i in ((gw_in, grad_in, 5), (gw_down, grad_down, 6)):
            made = pltpu.make_async_copy(src, dst, sems.at[i])
            made.start()
            stores.append(made)
    else:
        run_schedule([step for step in BACKWARD_0 if step != F], steps)
    net.finish()
    d_branch[...] = held[...]
    tally[...] = held_d[...]
    for made in stores:
        made.wait()
    if layer == 0:
        saving.wait()


def layer_backward(layer, lead, middle, gains, dense, kept, tokens, own_w, other_w):
    outs = [
        jax.ShapeDtypeStruct((OWN, WIDTH), F32),
        jax.ShapeDtypeStruct((RING, OWN, WIDTH), BF),
        jax.ShapeDtypeStruct((RING, OWN, 128), BF),
        jax.ShapeDtypeStruct((1, WIDTH), F32),
    ]
    kinds = [VM, VM, VM, VM]
    if layer == 1:
        outs += [
            jax.ShapeDtypeStruct((768, WIDTH), BF),
            jax.ShapeDtypeStruct((HIDDEN, WIDTH), BF),
        ]
        kinds += [ANY, ANY]
    else:
        outs += [
            jax.ShapeDtypeStruct((RING, RING, RING, OWN, 768), BF),
            jax.ShapeDtypeStruct((RING, RING, RING, OWN, HIDDEN), BF),
            jax.ShapeDtypeStruct(TOKENS_ALL, BF),
        ]
        kinds += [ANY, ANY, ANY]
    scratch = []
    lead_kinds = [Load((RING, OWN, WIDTH), of_pipe)]
    if layer == 0:
        lead_kinds = [LOAD] * 7 + [ANY] * 2
    if layer == 0:
        outs += [
            jax.ShapeDtypeStruct((RING, OWN, WIDTH), BF),
            jax.ShapeDtypeStruct((1, WIDTH), F32),
            jax.ShapeDtypeStruct((ROWS, QKV), BF),
            jax.ShapeDtypeStruct((8, 128), F32),
        ]
        kinds += [VM, VM, ANY, VM]
        scratch = [
            VM((RING, OWN, WIDTH), BF),
            VM((ROWS, QKV), BF),
            pltpu.SemaphoreType.DMA((3,)),
        ]
        scratch += state_scratch()
    scratch = scratch + [
        VM((OWN, WIDTH), BF),
        VM((RING, OWN, WIDTH), BF),
        VM((RING, OWN, 128), BF),
        VM(TOKENS_ALL, BF),
        VM(TOKENS_ALL, BF),
        VM(TOKENS_ALL, BF),
        VM((RING, RING, RING, OWN, 128), BF),
        VM((RING, RING, RING, OWN, HIDDEN), F32),
        VM((RING, RING, RING, OWN, 768), BF),
        VM((RING, RING, RING, OWN, HIDDEN), BF),
        VM((4, 192, WIDTH), BF),
        VM((2, 192, WIDTH), BF),
        VM((RING, RING, RING, OWN, 128), F32),
    ]
    if layer == 1:
        scratch += [VM((768, WIDTH), BF), VM((HIDDEN, WIDTH), BF), VM((HIDDEN, 2048), BF)]
    scratch += flat(reduce_scratch(3, TALLY_TILE)) + token_scratch()
    scratch += [pltpu.SemaphoreType.DMA((8,))]
    return call(
        functools.partial(layer_backward_kernel, layer),
        2 + 20 * layer,
        outs,
        lead_kinds + [LOAD] * 2 + [ANY] * 9,
        kinds,
        scratch,
        (
            *lead,
            middle,
            gains,
            dense,
            kept,
            tokens,
            *own_w,
            *other_w,
        ),
        12 + GATHER_COPIES + REDUCE_COPIES + 18 + 8 + 4,
        62,
    )


def body(
    inputs,
    cotangent,
    doc_bounds,
    routes,
    gates,
    norm_attn,
    norm_moe,
    q_gain,
    k_gain,
    w_query,
    key_matrix,
    value_matrix,
    w_out,
    w_gate,
    w_up,
    w_down,
):
    pipe = lax.axis_index("pipe")
    expert = lax.axis_index("expert")
    tensor = lax.axis_index("tensor")
    own_w = (w_gate[0], w_up[0], w_down[0])
    other_w = tuple(lax.ppermute(w, "pipe", [(0, 1), (1, 0)]) for w in own_w)

    named = routes[0][:, :, :, None] == jnp.arange(EXPERTS, dtype=jnp.int32)
    dense = jnp.sum(jnp.where(named, gates[0][:, :, :, None], 0.0), axis=2)
    dense = jnp.concatenate([dense[0], dense[1], jnp.zeros((ROWS, 64), F32)], axis=1)
    dense = dense.reshape(RING, OWN, 128)
    attn_0, attn_1, dense_all, gains, *layout = weight_gather(
        doc_bounds,
        w_query[0],
        key_matrix[0],
        value_matrix[0],
        w_out[0],
        dense,
        norm_attn,
        norm_moe,
        q_gain,
        k_gain,
    )
    first = pipe == 0

    kept, states = [], [inputs]
    by_rows = (RING, RING, RING, OWN, ATT)
    rows_0, rows_1 = attn_0.reshape(by_rows), attn_1.reshape(by_rows)
    weights_of = [(rows_0, rows_0), None]
    for layer in range(2):
        tokens, middle, both, state, normed, qkv, attended, *came = layer_forward(
            layer,
            states[layer],
            gains,
            dense_all,
            layout,
            weights_of[layer],
            own_w,
            other_w,
            *[attn_1][layer:],
        )
        if layer == 0:
            weights_of[1] = (came[0].reshape(by_rows), rows_1)
        kept.append((normed, qkv, attended, middle, tokens, both))
        states.append(state.reshape(ROWS, WIDTH))

    results, gain_sums = [None, None], [None, None]
    d_branch, d_qkv = [None, None], [None, None]
    for layer in (1, 0):
        normed, qkv, attended, middle, tokens, both = kept[layer]
        if layer == 1:
            lead = (cotangent.reshape(2, RING, OWN, WIDTH),)
        else:
            lead = (
                states[1].reshape(RING, OWN, WIDTH),
                dmid,
                d_branch[1],
                kept[1][1],
                *layout,
                *weights_of[1],
            )
        dmid, d_branch[layer], tally, d_norm_m, *more = layer_backward(
            layer, lead, middle, gains, dense_all, both, tokens, own_w, other_w
        )
        results[layer] = [
            normed,
            attended,
            d_branch[layer].reshape(ROWS, WIDTH),
            *more[: 2 * layer],
            states[layer + 1],
            tally.reshape(ROWS, 128),
        ]
        gain_sums[layer] = d_norm_m
    *stored, given_1, gain_1, d_qkv_1, d_gains_1 = more
    results[1].insert(1, d_qkv_1)
    attn_grad, given_0, total, in_came, down_came, act_came, tally_came, given_came, *grads_0 = tail(
        inputs,
        dmid,
        gains,
        d_branch[0],
        kept[0][1],
        layout,
        (gain_sums[0], gain_1, gain_sums[1], d_gains_1),
        weights_of[0],
        results,
        given_1,
        (*stored, kept[0][4]),
    )
    (d_gate, d_up, d_down, acts, givens, d_query, d_key, d_value, d_out, *d_gains) = write_outputs(
        attn_grad,
        total,
        grads_0[0],
        results[1][4],
        in_came,
        grads_0[1],
        results[1][5],
        down_came,
        states[1],
        states[2],
        act_came,
        given_0.reshape(ROWS, WIDTH),
        given_1.reshape(ROWS, WIDTH),
        given_came.reshape(ROWS, WIDTH),
    )
    tally = jnp.where(first, results[0][4], results[1][7])
    tally = jnp.where(first, jnp.stack([tally, tally_came]), jnp.stack([tally_came, tally]))
    tally = tally.astype(F32)[:, :, :EXPERTS]
    d_gates = jnp.sum(jnp.where(named, tally[:, :, None, :], 0.0), axis=3)
    return (
        acts[None],
        givens[None],
        *d_gains,
        d_query[None],
        d_key[None],
        d_value[None],
        d_out[None],
        *(grad.reshape(1, 2, 192, WIDTH) for grad in (d_gate, d_up, d_down)),
        d_gates[None],
    )


def solution(mesh):
    placed = (
        P(None, "expert", None),
        P(None, "expert", None),
        P(None, "expert", None),
        P("pipe", None, "expert", None),
        P("pipe", None, "expert", None),
        P("pipe", None),
        P("pipe", None),
        P("pipe", None),
        P("pipe", None),
        P("pipe", "expert", "tensor"),
        P("pipe", "expert", "tensor"),
        P("pipe", "expert", "tensor"),
        P("pipe", "tensor", "expert"),
        P("pipe", "expert", "tensor", None),
        P("pipe", "expert", "tensor", None),
        P("pipe", "expert", "tensor", None),
    )
    return jax.shard_map(
        body,
        mesh=mesh,
        in_specs=placed,
        out_specs=(
            P("pipe", None, "expert", None),
            P("pipe", None, "expert", None),
            P("pipe", None),
            P("pipe", None),
            P("pipe", None),
            P("pipe", None),
            P("pipe", "expert", "tensor"),
            P("pipe", "expert", "tensor"),
            P("pipe", "expert", "tensor"),
            P("pipe", "tensor", "expert"),
            P("pipe", "expert", "tensor", None),
            P("pipe", "expert", "tensor", None),
            P("pipe", "expert", "tensor", None),
            P("pipe", None, "expert", None),
        ),
        check_vma=False,
    )
```

```python
import functools
import math

import jax
import jax.numpy as jnp
from jax import lax
from jax.experimental import pallas as pl
from jax.experimental.pallas import tpu as pltpu
from jax.sharding import PartitionSpec as P

MESH = pl.DeviceIdType.MESH
ANY = pl.ANY
VM = pltpu.VMEM
F32 = jnp.float32
BF = jnp.bfloat16

HEAD_SIZE = 128
TOPK = 8
RING = 4
ROWS = 128
OWN = 32
WIDTH = 2048
HIDDEN = 384
QKV = 1280
ATT = 2304
EXPERTS = 32
GAIN_ROWS = 40
eps = 1e-06
rope_base = 1000000.0

ORDERS = (("y", "x", "z"), ("x", "z", "y"), ("z", "y", "x"))
CUTS = (
    ((0, 768), (768, 640), (1408, 640)),
    ((0, 640), (640, 768), (1408, 640)),
)
WORDERS = (("x", "z"), ("z", "x"))
WCUTS = ((0, 1152), (1152, 1152))


class Tile:
    def __init__(self, r0, rows, c0, cols, by_rows):
        self.r0, self.rows, self.c0, self.cols, self.by_rows = r0, rows, c0, cols, by_rows
        if by_rows:
            first = rows // 2
            self.spans = {
                None: (0, rows, 0, cols),
                0: (0, first, 0, cols),
                1: (first, rows - first, 0, cols),
            }
        else:
            first = (cols // 128 + 1) // 2 * 128
            self.spans = {
                None: (0, rows, 0, cols),
                0: (0, rows, 0, first),
                1: (0, rows, first, cols - first),
            }

    def shape(self, half=None):
        _, rows, _, cols = self.spans[half]
        return (rows, cols)

    def at(self, half=None):
        r, rows, c, cols = self.spans[half]
        return (pl.ds(self.r0 + r, rows), pl.ds(self.c0 + c, cols))

    def own(self):
        return Tile(0, self.rows, 0, self.cols, self.by_rows)


class Place:
    def __init__(self):
        self.pipe = lax.axis_index("pipe")
        expert = lax.axis_index("expert")
        self.at = {
            "z": lax.div(expert, RING),
            "x": lax.rem(expert, RING),
            "y": lax.axis_index("tensor"),
        }

    def step(self, axis, by):
        return lax.rem(self.at[axis] + (by + RING), RING)

    def device(self, axis, by):
        at = dict(self.at)
        at[axis] = self.step(axis, by)
        return (self.pipe, at["z"] * RING + at["x"], at["y"])

    def sibling(self):
        return (1 - self.pipe, self.at["z"] * RING + self.at["x"], self.at["y"])


class Net:
    def __init__(self, send, recv, base=0):
        self.send, self.recv, self.base, self.made = send, recv, base, []

    def describe(self, src, dst, device, i):
        return pltpu.make_async_remote_copy(
            src_ref=src,
            dst_ref=dst,
            send_sem=self.send.at[self.base + i],
            recv_sem=self.recv.at[self.base + i],
            device_id=device,
            device_id_type=MESH,
        )

    def copy(self, src, dst, device):
        made = self.describe(src, dst, device, len(self.made))
        made.start()
        self.made.append(made)
        return made

    def finish(self):
        for made in self.made:
            made.wait_send()


def greet(devices, before_wait=None):
    barrier = pltpu.get_barrier_semaphore()
    for device in devices:
        pl.semaphore_signal(barrier, inc=1, device_id=device, device_id_type=MESH)
    wait_loads()
    if before_wait is not None:
        before_wait()
    pl.semaphore_wait(barrier, len(devices))


def greet_sibling(place, devices, before_wait):
    barrier = pltpu.get_barrier_semaphore()
    for device in devices:
        pl.semaphore_signal(barrier, inc=1, device_id=device, device_id_type=MESH)

    @pl.when(place.pipe == 0)
    def _():
        pl.semaphore_signal(barrier, inc=1, device_id=place.sibling(), device_id_type=MESH)

    wait_loads()
    before_wait()

    @pl.when(place.pipe == 0)
    def _():
        pl.semaphore_wait(barrier, len(devices))

    @pl.when(place.pipe == 1)
    def _():
        pl.semaphore_wait(barrier, len(devices) + 1)


def around(place, axes):
    return [place.device(axis, by) for axis in axes for by in (1, -1)]


def together(steps):
    for _ in in_turn(steps):
        pass


def in_turn(steps):
    live = list(steps)
    while live:
        kept = []
        for step in live:
            try:
                next(step)
                kept.append(step)
            except StopIteration:
                pass
        live = kept
        if live:
            yield


def gather_ring(net, place, axis, block, first=None, seen=None):
    me, left, right, far = (place.step(axis, by) for by in (0, -1, 1, 2))
    mine = block(me, None) if first is None else first
    to_right = net.copy(mine, block(me, None), place.device(axis, 1))
    to_left = net.copy(mine, block(me, None), place.device(axis, -1))
    yield
    to_right.wait_recv()
    on_right = net.copy(block(left, 0), block(left, 0), place.device(axis, 1))
    to_left.wait_recv()
    on_left = net.copy(block(right, 1), block(right, 1), place.device(axis, -1))
    if seen is not None:
        seen(left)
        seen(right)
    yield
    on_right.wait_recv()
    on_left.wait_recv()
    if seen is not None:
        seen(far)


def gather_all(net, place, order, block, first):
    wanted = {axis: place.at[axis] for axis in order}
    for number, axis in enumerate(order):
        held = dict(wanted)

        def part(i, half, held=held, axis=axis):
            return block({**held, axis: i}, half)

        yield from gather_ring(net, place, axis, part, first if number == 0 else None)
        wanted[axis] = None


SUBS = [(chunk, sub) for chunk in range(3) for sub in range(2)]
TILES = {
    (chunk, sub): Tile(sub * 16, 16, *CUTS[sub][chunk], False) for chunk, sub in SUBS
}
TALLY_TILE = Tile(0, OWN, 0, 128, True)
STATE_TILES = [Tile(lo, 16, 0, WIDTH, False) for lo in (0, 16)]
WSUBS = [(chunk, sub) for chunk in range(2) for sub in range(2)]
WTILES = {
    (chunk, sub): Tile(sub * 64, 64, WCUTS[chunk][0], WCUTS[chunk][1], True)
    for chunk, sub in WSUBS
}


def add_into(out, terms, shape):
    def tile(spot):
        summed = terms[0][spot]
        for term in terms[1:]:
            summed = summed + term[spot]
        out[spot] = summed

    lead, rows = shape[:-2], shape[-2]
    if len(lead) == 2:

        def each(i, _):
            tile((i, slice(None), slice(None), slice(None)))
            return 0

        lax.fori_loop(0, lead[0], each, 0)
    elif rows <= OWN:
        tile((slice(None),) * len(shape))
    else:
        tiles = rows // OWN

        def each(i, _):
            spot = (pl.ds(pl.multiple_of(lax.rem(i, tiles) * OWN, OWN), OWN), slice(None))
            tile((lax.div(i, tiles),) * len(lead) + spot)
            return 0

        lax.fori_loop(0, tiles * (lead[0] if lead else 1), each, 0)


def ring_scratch(lead, tile):
    return [
        VM(lead + tile.shape(0), BF),
        VM(lead + tile.shape(1), BF),
        VM(lead + tile.shape(), BF),
        VM(lead + tile.shape(), BF),
    ]


def reduce_ring(net, place, axis, block, lead, tile, bufs, make=None):
    near_left, near_right, from_left, from_right = bufs
    whole = (slice(None),) * len(lead)

    def half_of(ref, half):
        return ref.at[whole + tile.own().at(half)]

    me, left, right, far = (place.step(axis, by) for by in (0, -1, 1, 2))
    go_right, go_left = place.device(axis, 1), place.device(axis, -1)
    if make is not None:
        make(2)
    far_right = net.copy(block(far, 0), near_left, go_right)
    far_left = net.copy(block(far, 1), near_right, go_left)
    if make is not None:
        yield
        make(1)
    own_right = net.copy(block(right, 1), half_of(from_left, 1), go_right)
    if make is not None:
        make(-1)
    own_left = net.copy(block(left, 0), half_of(from_right, 0), go_left)
    yield
    far_right.wait_recv()
    add_into(near_left, [near_left, block(right, 0)], lead + tile.shape(0))
    sum_right = net.copy(near_left, half_of(from_left, 0), go_right)
    far_left.wait_recv()
    add_into(near_right, [near_right, block(left, 1)], lead + tile.shape(1))
    sum_left = net.copy(near_right, half_of(from_right, 1), go_left)
    yield
    if make is not None:
        make(0)
    for made in (own_right, sum_right, own_left, sum_left):
        made.wait_recv()
    add_into(from_left, [from_left, block(me, None), from_right], lead + tile.shape())


def reduce_all(net, place, order, names, source, tile, bufs, make=None):
    left = [name for name in names]
    for number, axis in enumerate(order):
        spot = left.index(axis)
        lead = tuple(RING for _ in left[1:])
        if number == 0:
            block = lambda i, half, axis=axis: source({axis: i}, half)
        else:
            prior = bufs[number - 1][2]

            def block(i, half, prior=prior, spot=spot, count=len(left)):
                where = [slice(None)] * count
                where[spot] = i
                return prior.at[tuple(where) + tile.own().at(half)]

        yield from reduce_ring(
            net, place, axis, block, lead, tile, bufs[number], make if number == 0 else None
        )
        left.remove(axis)


def reduce_scratch(order_count, tile):
    return [
        ring_scratch((RING,) * (order_count - 1 - number), tile) for number in range(order_count)
    ]


def take(refs, structure):
    return [take(refs, part) if isinstance(part, list) else refs.pop(0) for part in structure]


def flat(structure):
    return [leaf for part in structure for leaf in (flat(part) if isinstance(part, list) else [part])]


def token_block(ref, tile):
    def block(wanted, half):
        where = tuple(slice(None) if wanted.get(a) is None else wanted[a] for a in ("z", "x", "y"))
        return ref.at[where + tile.at(half)]

    return block


def gather_tokens(net, place, stream, own, out):
    return in_turn(
        [
            gather_all(
                net,
                place,
                ORDERS[chunk],
                token_block(out, TILES[chunk, stream]),
                own.at[TILES[chunk, stream].at()],
            )
            for chunk in range(3)
        ]
    )


def inv_rms(values):
    return lax.rsqrt(jnp.mean(values * values, axis=-1, keepdims=True) + eps)


def tensor_blocks(ref, tile):
    def block(i, half):
        return ref.at[(i,) + tile.at(half)]

    return block


def reduce_tensor(net, place, stream, part, bufs):
    tile = STATE_TILES[stream]
    return reduce_ring(net, place, "y", tensor_blocks(part, tile), (), tile, bufs[stream])


def gather_tensor(net, place, stream, held):
    return gather_ring(net, place, "y", tensor_blocks(held, STATE_TILES[stream]))


def state_scratch():
    return flat([ring_scratch((), tile) for tile in STATE_TILES])


def state_bufs(refs):
    return take(list(refs), [[None] * 4, [None] * 4])


def norm_back(dy, values, gain):
    scale = inv_rms(values)
    weighted = dy * gain
    back = scale * weighted - values * (scale * scale * scale) * jnp.mean(
        weighted * values, axis=-1, keepdims=True
    )
    return back, dy * values * scale


TOKENS_ALL = (RING, RING, RING, OWN, WIDTH)
GATHER_COPIES = 4 * 9 * 2
REDUCE_COPIES = 6 * 9 * 2


class Load:
    def __init__(self, shape=None, pick=None):
        self.shape, self.pick = shape, pick or (lambda ref: ref)


LOAD = Load()
LOADING = []


def wait_loads():
    while LOADING:
        LOADING.pop().wait()


def loading(kernel, kinds, args):
    loads = [i for i, kind in enumerate(kinds) if isinstance(kind, Load)]
    scratch = [VM(kinds[i].shape or args[i].shape, args[i].dtype) for i in loads]
    scratch.append(pltpu.SemaphoreType.DMA((len(loads),)))

    def wrapped(*refs):
        refs, held, sems = list(refs[: -len(loads) - 1]), refs[-len(loads) - 1 : -1], refs[-1]
        for k, i in enumerate(loads):
            made = pltpu.make_async_copy(kinds[i].pick(refs[i]), held[k], sems.at[k])
            made.start()
            LOADING.append(made)
            refs[i] = held[k]
        kernel(*refs)

    return wrapped, scratch, [ANY if isinstance(kind, Load) else kind for kind in kinds]


def call(kernel, ident, shapes, in_kinds, out_kinds, scratch, args, copies, vmem=60):
    kernel, held, in_kinds = loading(kernel, in_kinds, args)
    return pl.pallas_call(
        kernel,
        out_shape=shapes,
        in_specs=[pl.BlockSpec(memory_space=kind) for kind in in_kinds],
        out_specs=[pl.BlockSpec(memory_space=kind) for kind in out_kinds],
        scratch_shapes=scratch
        + [pltpu.SemaphoreType.DMA((copies,)), pltpu.SemaphoreType.DMA((copies,))]
        + held,
        compiler_params=pltpu.CompilerParams(
            collective_id=ident, has_side_effects=True, vmem_limit_bytes=vmem * 2**20
        ),
    )(*args)


def of_pipe(ref):
    return ref.at[lax.axis_index("pipe")]


def with_sem(kernel):
    def inner(*refs):
        return kernel(*refs[:-3], refs[-2], refs[-1], refs[-3])

    return inner


def reduce_tokens(net, place, stream, part, bufs, make):
    return in_turn(
        [
            reduce_all(
                net,
                place,
                ORDERS[chunk][::-1],
                ("z", "x", "y"),
                token_block(part, TILES[chunk, stream]),
                TILES[chunk, stream],
                bufs[chunk, stream],
                functools.partial(make, chunk, stream),
            )
            for chunk in range(3)
        ]
    )


def token_scratch():
    return flat([reduce_scratch(3, TILES[sub]) for sub in SUBS])


def token_bufs(refs):
    return {sub: [[refs.pop(0) for _ in range(4)] for _ in range(3)] for sub in SUBS}


def token_sums(bufs, sub):
    return jnp.concatenate(
        [bufs[chunk, sub][-1][2][...].astype(F32) for chunk in range(3)], axis=-1
    )


def add_rows(out, rows):
    out[...] = out[...] + jnp.sum(rows, axis=0, keepdims=True)


def state_back(place, stream, base, dmid, gain, bufs, dgain, put):
    t = place.at["y"]
    rs = pl.ds(stream * 16, 16)
    summed = bufs[stream][2][...].astype(F32)
    back, rows = norm_back(summed, base[t, rs, :].astype(F32), gain[...])
    put(t, rs, (dmid[rs, :] + back).astype(BF))
    add_rows(dgain, rows)


def run_schedule(schedule, steps):
    for name in schedule:
        next(steps[name], None)
    together(steps.values())


DENSE_COPIES = 16
RING_COPIES = 32
PASS_COPIES = 28


def write_tables(bounds, pipe, cosine, sine, bias):
    start, end = bounds[pipe, 0, 0], bounds[pipe, 0, 1]
    row = lax.broadcasted_iota(jnp.int32, (ROWS, 128), 0)
    lane = lax.broadcasted_iota(jnp.int32, (ROWS, 128), 1)
    first = jnp.where(row >= end, end, jnp.where(row >= start, start, 0))
    past = jnp.where(row >= end, ROWS, jnp.where(row >= start, end, start))
    bias[...] = jnp.where((lane >= first) & (lane <= row) & (lane < past), 0.0, -1e30)
    half = jnp.where(lane < 64, lane, lane - 64).astype(F32)
    freqs = jnp.exp(half * (-2.0 / HEAD_SIZE * math.log(rope_base)))
    angles = (row - first).astype(F32) * freqs
    cosine[...] = jnp.cos(angles)
    sine[...] = jnp.where(lane < 64, -1.0, 1.0) * jnp.sin(angles)


def weight_gather_kernel(*refs):
    (bounds, w_q, w_k, w_v, w_o, dense, norm_a, norm_m, q_gain, k_gain) = refs[:10]
    (attn_0, attn_1, dense_all, gains_all, cosine, sine, bias) = refs[10:17]
    shard, gains, send, recv, sems = refs[17:]
    place = Place()
    sib = place.sibling()
    p, z, x = place.pipe, place.at["z"], place.at["x"]
    wait_loads()
    shard[:, pl.ds(0, 1024)] = w_q[...]
    shard[:, pl.ds(1024, 128)] = w_k[...]
    shard[:, pl.ds(1152, 128)] = w_v[...]
    shard[:, pl.ds(QKV, 1024)] = w_o[...].T
    gains[...] = jnp.zeros((8, WIDTH), F32)
    gains[pl.ds(0, 1), :] = norm_a[...]
    gains[pl.ds(1, 1), :] = norm_m[...]
    gains[pl.ds(2, 1), pl.ds(0, 128)] = q_gain[...]
    gains[pl.ds(2, 1), pl.ds(128, 128)] = k_gain[...]
    greet(around(place, "xz") + [sib])

    def attn_block(attn, tile):
        def block(wanted, half):
            where = tuple(slice(None) if wanted[a] is None else wanted[a] for a in ("z", "x"))
            return attn.at[where + tile.at(half)]

        return block

    def dense_block(wanted, half):
        where = (p,) + tuple(slice(None) if wanted[a] is None else wanted[a] for a in ("z", "x"))
        rs = slice(None) if half is None else pl.ds(half * 2, 2)
        return dense_all.at[where + (rs,)]

    def run(net, order, block, first, seen):
        wanted = {axis: place.at[axis] for axis in order}
        for number, axis in enumerate(order):
            held = dict(wanted)

            def part(i, half, held=held, axis=axis):
                return block({**held, axis: i}, half)

            yield from gather_ring(
                net,
                place,
                axis,
                part,
                first if number == 0 else None,
                None if seen is None else functools.partial(seen, number, part),
            )
            wanted[axis] = None

    def dense_run(net):
        passed = [net.copy(dense, dense_all.at[p, z, x], sib), net.copy(gains, gains_all.at[p], sib)]

        def seen(number, part, i):
            passed.append(net.copy(part(i, None), part(i, None), sib))

        yield from run(net, ("x", "z"), dense_block, dense, seen)
        for made in passed:
            made.wait_recv()

    placed = [
        pltpu.make_async_copy(dense, dense_all.at[p, z, x], sems.at[0]),
        pltpu.make_async_copy(gains, gains_all.at[p], sems.at[1]),
    ]
    for made in placed:
        made.start()
    placed[0].wait()
    def rings(net, attn, seen):
        return [
            run(
                net,
                WORDERS[sub[0]],
                attn_block(attn, WTILES[sub]),
                shard.at[WTILES[sub].at()],
                None if seen is None else functools.partial(seen, i),
            )
            for i, sub in enumerate(WSUBS)
        ]

    def own_block(attn, tile):
        return attn.at[(z, x) + tile.at()]

    @pl.when(p == 0)
    def _():
        net_d = Net(send, recv)
        net_w = Net(send, recv, DENSE_COPIES)
        passing = Net(send, recv, DENSE_COPIES + RING_COPIES)
        made = pltpu.make_async_copy(shard, attn_0.at[z, x], sems.at[2])
        made.start()
        counts = [0] * len(WSUBS)

        def pass_on(sub, number, part, i):
            at = sub * 7 + 1 + counts[sub]
            counts[sub] += 1
            crossing = passing.describe(part(i, None), part(i, None), sib, at)
            crossing.start()
            passing.made.append(crossing)

        steps = rings(net_w, attn_0, pass_on)
        for step in steps:
            next(step)
        write_tables(bounds, p, cosine, sine, bias)
        for i, sub in enumerate(WSUBS):
            crossing = passing.describe(
                shard.at[WTILES[sub].at()], own_block(attn_0, WTILES[sub]), sib, i * 7
            )
            crossing.start()
            passing.made.append(crossing)
        made.wait()
        together(steps + [dense_run(net_d)])
        for net in (net_d, net_w, passing):
            net.finish()

    @pl.when(p == 1)
    def _():
        net_d = Net(send, recv)
        net_w = Net(send, recv, DENSE_COPIES)
        passing = Net(send, recv, DENSE_COPIES + RING_COPIES)
        made = pltpu.make_async_copy(shard, attn_1.at[z, x], sems.at[2])
        made.start()
        write_tables(bounds, p, cosine, sine, bias)
        together([dense_run(net_d)])

        def receive(number):
            for i, sub in enumerate(WSUBS):
                order = WORDERS[sub[0]]
                wanted = {axis: place.at[axis] for axis in order}
                if number == 0:
                    spot = own_block(attn_0, WTILES[sub])
                    passing.describe(spot, spot, sib, i * 7).wait_recv()
                else:
                    wanted[order[0]] = None
                for k, by in enumerate((-1, 1, 2)):
                    axis = order[number]
                    spot = attn_block(attn_0, WTILES[sub])(
                        {**wanted, axis: place.step(axis, by)}, None
                    )
                    passing.describe(spot, spot, sib, i * 7 + 1 + 3 * number + k).wait_recv()

        receive(0)
        made.wait()
        steps = rings(net_w, attn_1, None)
        for step in steps:
            next(step)
        receive(1)
        together(steps)
        for net in (net_d, net_w):
            net.finish()

    placed[1].wait()


def weight_gather(*args):
    attn = jax.ShapeDtypeStruct((RING, RING, ROWS, ATT), BF)
    table = jax.ShapeDtypeStruct((ROWS, 128), F32)
    return call(
        with_sem(weight_gather_kernel),
        7,
        [
            attn,
            attn,
            jax.ShapeDtypeStruct((2, RING, RING, RING, OWN, 128), F32),
            jax.ShapeDtypeStruct((2, 8, WIDTH), F32),
            table,
            table,
            table,
        ],
        [pltpu.SMEM] + [LOAD] * 9,
        [ANY] * 4 + [VM] * 3,
        [
            VM((ROWS, ATT), BF),
            VM((8, WIDTH), F32),
            pltpu.SemaphoreType.DMA((3,)),
        ],
        args,
        DENSE_COPIES + RING_COPIES + PASS_COPIES,
    )


def sum_everywhere(net, place, value, slots, pair, total):
    current = value[...]
    for number, axis in enumerate("yxz"):
        slot = slots.at[number]
        slot[place.at[axis]] = current

        def block(i, half, slot=slot):
            return slot.at[i] if half is None else slot.at[i, pl.ds(half, 1)]

        yield from gather_ring(net, place, axis, block)
        current = (slot[0] + slot[1]) + (slot[2] + slot[3])
    pair[place.pipe] = current
    crossed = net.copy(pair.at[place.pipe], pair.at[place.pipe], place.sibling())
    yield
    crossed.wait_recv()
    total[...] = pair[0] + pair[1]


TAIL_COPIES = 12 + 8 + 13 + 48
TRADES = 9
TAIL_SUBS = [
    (order[::-1], Tile(0, ROWS, lo, width, True))
    for order, lo, width in (
        (WORDERS[0], 1280, 512),
        (WORDERS[1], 1792, 512),
        (WORDERS[0], 0, 640),
        (WORDERS[1], 640, 640),
    )
]


def tail_kernel(*refs):
    refs = list(refs)
    base, dmid, gains, d_branch_0, qkv_0 = refs[:5]
    tables, gain_rows, on_core = refs[5:8], refs[8:12], refs[12:14]
    gain = gains.at[0, pl.ds(0, 1)]
    by_layer = [refs[14:19], refs[19:27]]
    given_1, stored = refs[27], refs[28:32]
    out, given_0, total = refs[32:35]
    came = refs[35:39]
    came_given, grads_out = refs[39], refs[40:42]
    part, d_qkv_v, d_gains = refs[42:45]
    both, hidden, g_all, x_all, gw_in, gw_down, turned = refs[45:52]
    attn_sems, refs = refs[52], refs[53:]
    by_layer[0].insert(1, d_qkv_v)
    by_layer[0][4:4] = [gw_in, gw_down]
    near, refs = state_bufs(refs[:8]), refs[8:]
    held, ops, part_w = refs[0], refs[1:5], refs[5]
    *bufs, slots, pair, value_v, tally, sems, send, recv = refs[6:]
    bufs = [[[bufs.pop(0) for _ in range(4)] for _ in range(2)] for sub in TAIL_SUBS]
    place = Place()
    sib = place.sibling()
    net = Net(send, recv)
    trade = Net(send, recv, TAIL_COPIES)
    mine, theirs = pl.ds(0, ROWS), pl.ds(ROWS, ROWS)
    targets = [op.at[theirs] for op in ops] + list(came)

    def owed(layer, which):
        return [
            trade.describe(by_layer[layer][i], targets[i], sib, i) for i in which
        ]

    w_out, w_qkv = g_all.at[EVERY + (pl.ds(0, 1024),)], x_all.at[EVERY + (pl.ds(0, QKV),)]
    fetched_w = fetch_attention(on_core, [(QKV, w_out), (0, w_qkv)], attn_sems)

    def exchange(which):
        for core in range(2):

            @pl.when(place.pipe == core)
            def _(core=core):
                for i in which:
                    pltpu.make_async_copy(by_layer[core][i], ops[i].at[mine], sems.at[i]).start()
                for made in owed(1 - core, which):
                    made.start()

    greet(around(place, "xyz") + [sib])
    exchange((2, 3))
    attention_backward(
        0,
        d_branch_0,
        qkv_0,
        fetched_w,
        w_out,
        w_qkv,
        gains,
        tables,
        part,
        d_qkv_v,
        d_gains,
    )
    exchange((0, 1))
    loads = [
        pltpu.make_async_copy(src, dst, attn_sems.at[2 + i])
        for i, (src, dst) in enumerate(zip(stored, (both, hidden, g_all, x_all)))
    ]
    for made in loads:
        made.start()
    value_v[...] = jnp.zeros((2, GAIN_ROWS, 128), F32)
    for layer, row, source in ((0, 16, 0), (1, 0, 1), (1, 16, 2)):
        for i in range(16):
            value_v[layer, pl.ds(row + i, 1), :] = gain_rows[source][:, pl.ds(i * 128, 128)]
    value_v[0, pl.ds(32, 8), :] = d_gains[...]
    value_v[1, pl.ds(32, 8), :] = gain_rows[3][...]
    tally[...] = jnp.zeros((1, WIDTH), F32)

    def state_run():
        def put(t, rs, rows):
            held[t, rs, :] = rows

        yield from in_turn([reduce_tensor(net, place, stream, part, near) for stream in range(2)])
        for stream in range(2):
            state_back(place, stream, base, dmid, gain, near, tally, put)
        for i in range(16):
            value_v[0, pl.ds(i, 1), :] = tally[:, pl.ds(i * 128, 128)]
        yield from in_turn([gather_tensor(net, place, stream, held) for stream in range(2)])

        @pl.when(place.pipe == 1)
        def _():
            trade.describe(held, came_given, sib, 8).start()

        yield from sum_everywhere(net, place, value_v, slots, pair, total)

    state_step = state_run()
    next(state_step)
    steps = []

    def start_reduce(which):
        for sub in which:
            order, tile = TAIL_SUBS[sub]

            def source(wanted, half, tile=tile):
                where = tuple(wanted.get(a, slice(None)) for a in ("z", "x"))
                return part_w.at[where + tile.at(half)]

            step = reduce_all(net, place, order, ("z", "x"), source, tile, bufs[sub])
            next(step)
            steps.append(step)

    for left, right, lo, width, subs in ((3, 2, QKV, 1024, (0, 1)), (0, 1, 0, QKV, (2, 3))):
        for i in (left, right):
            pltpu.make_async_copy(by_layer[0][i], ops[i].at[mine], sems.at[i]).wait()
            trade.describe(ops[i].at[theirs], targets[i], sib, i).wait_recv()

        def product(i, _, left=left, right=right, lo=lo, width=width):
            dims = pl.ds(pl.multiple_of(i * 512, 512), 512)
            made = dot_tn(ops[left][:, dims], ops[right][...]).astype(BF)
            part_w[i, :, :, pl.ds(lo, width)] = made.reshape(RING, ROWS, width)
            return 0

        lax.fori_loop(0, RING, product, 0)
        start_reduce(subs)
    for made in loads:
        made.wait()
    fill = weight_grads(
        ((hidden, 0, g_all, gw_down), (both, 0, x_all, gw_in), (both, HIDDEN, x_all, gw_in)), turned
    )
    for number in range(6):
        next(fill)
        if number % 2:
            next(state_step)
    for step in steps:
        next(step)
    for number in range(6):
        next(fill)
        if number % 2:
            next(state_step)
    stores = [
        pltpu.make_async_copy(src, dst, attn_sems.at[i])
        for i, (src, dst) in enumerate(zip((gw_in, gw_down), grads_out))
    ]
    for made in stores:
        made.start()
    for core in range(2):

        @pl.when(place.pipe == core)
        def _(core=core):
            for made in owed(1 - core, range(4, 8)):
                made.start()
            if core == 0:
                trade.describe(given_1, came_given, sib, 8).start()

    together([state_step] + steps)
    for (_, tile), buf in zip(TAIL_SUBS, bufs):
        out[tile.at()] = buf[-1][2][...].astype(F32)
    given_0[...] = held[...]
    net.finish()
    for core in range(2):

        @pl.when(place.pipe == core)
        def _(core=core):
            for made in owed(1 - core, range(8)):
                made.wait_send()
            source = given_1 if core == 0 else held
            trade.describe(source, came_given, sib, 8).wait_send()

    for made in stores:
        made.wait()
    for i in range(4, 8):
        trade.describe(targets[i], targets[i], sib, i).wait_recv()
    trade.describe(came_given, came_given, sib, 8).wait_recv()


def tail(base, dmid, gains, d_branch, qkv, tables, gain_rows, on_core, by_layer, given_1, stored):
    shapes = [x.shape for x in by_layer[1]]
    return call(
        tail_kernel,
        8,
        [
            jax.ShapeDtypeStruct((ROWS, ATT), F32),
            jax.ShapeDtypeStruct((RING, OWN, WIDTH), BF),
            jax.ShapeDtypeStruct((2, GAIN_ROWS, 128), F32),
        ]
        + [jax.ShapeDtypeStruct(shape, BF) for shape in shapes[4:]]
        + [jax.ShapeDtypeStruct((RING, OWN, WIDTH), BF)]
        + [jax.ShapeDtypeStruct((768, WIDTH), BF), jax.ShapeDtypeStruct((HIDDEN, WIDTH), BF)],
        [Load((RING, OWN, WIDTH), of_pipe)] + [LOAD] * 11 + [ANY] * 20,
        [VM] * 3 + [ANY] * 7,
        [
            VM((RING, OWN, WIDTH), BF),
            VM((ROWS, QKV), BF),
            VM((8, 128), F32),
            VM((RING, RING, RING, OWN, 768), BF),
            VM((RING, RING, RING, OWN, HIDDEN), BF),
            VM(TOKENS_ALL, BF),
            VM(TOKENS_ALL, BF),
            VM((768, WIDTH), BF),
            VM((HIDDEN, WIDTH), BF),
            VM((HIDDEN, 2048), BF),
            pltpu.SemaphoreType.DMA((6,)),
        ]
        + state_scratch()
        + [VM((RING, OWN, WIDTH), BF)]
        + [VM((2 * ROWS, shape[1]), BF) for shape in shapes[:4]]
        + [VM((RING, RING, ROWS, ATT), BF)]
        + flat([reduce_scratch(2, tile) for _, tile in TAIL_SUBS])
        + [
            VM((3, RING, 2, GAIN_ROWS, 128), F32),
            VM((2, 2, GAIN_ROWS, 128), F32),
            VM((2, GAIN_ROWS, 128), F32),
            VM((1, WIDTH), F32),
            pltpu.SemaphoreType.DMA((4,)),
        ],
        (
            base.reshape(2, RING, OWN, WIDTH),
            dmid,
            gains,
            d_branch,
            qkv,
            *tables,
            *gain_rows,
            *on_core,
            *by_layer[0],
            *by_layer[1],
            given_1,
            *stored,
        ),
        TAIL_COPIES + TRADES,
    )


def write_kernel(*refs):
    refs = list(refs)
    attn, total = refs[:2]
    in_0, in_1, in_came, down_0, down_1, down_came = refs[2:8]
    act_0, act_1, act_came, given_0, given_1, given_came = refs[8:14]
    d_gate, d_up, d_down, acts, givens, d_query, d_key, d_value, d_out = refs[14:23]
    d_norm_a, d_norm_m, d_q, d_k = refs[23:27]
    pieces, pieces_came, sums, rows, rows_f, sem_in, sem_out = refs[27:]
    pipe = lax.axis_index("pipe")
    adds = []

    def load(i):
        which, lo = divmod(i * 192, HIDDEN)
        own = (in_0, in_1) if which < 2 else (down_0, down_1)
        came = in_came if which < 2 else down_came
        rs = pl.ds(lo + (HIDDEN if which == 1 else 0), 192)
        for core in range(2):

            @pl.when(pipe == core)
            def _(source=own[core]):
                pltpu.make_async_copy(source.at[rs], pieces.at[i], sem_in.at[2 * i]).start()

        pltpu.make_async_copy(came.at[rs], pieces_came.at[i], sem_in.at[2 * i + 1]).start()
        adds.append((d_gate, d_up, d_down)[which].at[pl.ds(lo, 192)])

    sources = ((act_0, act_1), (given_0, given_1))

    def load_rows(k):
        for core in range(2):

            @pl.when(pipe == core)
            def _(source=sources[k][core]):
                pltpu.make_async_copy(source, rows.at[2 * k], sem_in.at[12 + 2 * k]).start()

        came = (act_came, given_came)[k]
        pltpu.make_async_copy(came, rows.at[2 * k + 1], sem_in.at[13 + 2 * k]).start()

    for i in range(3):
        load(i)
    stores = []
    wait_loads()
    for i in range(16):
        d_norm_a[:, pl.ds(i * 128, 128)] = total[pipe, pl.ds(i, 1), :]
        d_norm_m[:, pl.ds(i * 128, 128)] = total[pipe, pl.ds(16 + i, 1), :]
    d_q[...] = total[pipe, pl.ds(32, 1), :]
    d_k[...] = total[pipe, pl.ds(33, 1), :]
    d_query[...] = attn[:, pl.ds(0, 1024)]
    d_key[...] = attn[:, pl.ds(1024, 128)]
    d_value[...] = attn[:, pl.ds(1152, 128)]
    d_out[...] = attn[:, pl.ds(QKV, 1024)].T
    for i in range(6):
        pltpu.make_async_copy(in_0.at[pl.ds(0, 192)], pieces.at[i], sem_in.at[2 * i]).wait()
        pltpu.make_async_copy(in_0.at[pl.ds(0, 192)], pieces_came.at[i], sem_in.at[2 * i + 1]).wait()
        if i < 3:
            load(i + 3)
        elif i < 5:
            load_rows(i - 3)

        def each(j, _, i=i):
            rs = pl.ds(pl.multiple_of(j * 32, 32), 32)
            sums[i, rs, :] = pieces[i, rs, :].astype(F32) + pieces_came[i, rs, :].astype(F32)
            return 0

        lax.fori_loop(0, 6, each, 0)
        made = pltpu.make_async_copy(sums.at[i], adds[i], sem_out.at[i])
        made.start()
        stores.append(made)
    for k, out in enumerate((acts, givens)):
        for n in range(2):
            i = 2 * k + n
            pltpu.make_async_copy(act_0, rows.at[i], sem_in.at[12 + i]).wait()

            def each(j, _, i=i):
                rs = pl.ds(pl.multiple_of(j * 16, 16), 16)
                rows_f[i, rs, :] = rows[i, rs, :].astype(F32)
                return 0

            lax.fori_loop(0, 8, each, 0)
            spot = out.at[pipe if n == 0 else 1 - pipe]
            made = pltpu.make_async_copy(rows_f.at[i], spot, sem_out.at[6 + i])
            made.start()
            stores.append(made)
    for made in stores:
        made.wait()


def write_outputs(*args):
    kernel, held, kinds = loading(write_kernel, [LOAD] * 2 + [ANY] * 12, args)
    return pl.pallas_call(
        kernel,
        out_shape=[jax.ShapeDtypeStruct((HIDDEN, WIDTH), F32)] * 3
        + [jax.ShapeDtypeStruct((2, ROWS, WIDTH), F32)] * 2
        + [
            jax.ShapeDtypeStruct((ROWS, 1024), F32),
            jax.ShapeDtypeStruct((ROWS, 128), F32),
            jax.ShapeDtypeStruct((ROWS, 128), F32),
            jax.ShapeDtypeStruct((1024, ROWS), F32),
            jax.ShapeDtypeStruct((1, WIDTH), F32),
            jax.ShapeDtypeStruct((1, WIDTH), F32),
            jax.ShapeDtypeStruct((1, 128), F32),
            jax.ShapeDtypeStruct((1, 128), F32),
        ],
        in_specs=[pl.BlockSpec(memory_space=kind) for kind in kinds],
        out_specs=[pl.BlockSpec(memory_space=ANY)] * 5 + [pl.BlockSpec(memory_space=VM)] * 8,
        scratch_shapes=[
            VM((6, 192, WIDTH), BF),
            VM((6, 192, WIDTH), BF),
            VM((6, 192, WIDTH), F32),
            VM((4, ROWS, WIDTH), BF),
            VM((4, ROWS, WIDTH), F32),
            pltpu.SemaphoreType.DMA((16,)),
            pltpu.SemaphoreType.DMA((10,)),
        ]
        + held,
        compiler_params=pltpu.CompilerParams(vmem_limit_bytes=60 * 2**20),
        cost_estimate=pl.CostEstimate(flops=0, bytes_accessed=24 * 2**20, transcendentals=0),
    )(*args)


def dot_nn(a, b):
    return lax.dot_general(a, b, (((1,), (0,)), ((), ())), preferred_element_type=F32)


def dot_nt(a, b):
    return lax.dot_general(a, b, (((1,), (1,)), ((), ())), preferred_element_type=F32)


def dot_tn(a, b):
    return lax.dot_general(a, b, (((0,), (0,)), ((), ())), preferred_element_type=F32)


def stack_heads(values, count):
    return jnp.concatenate([values[:, h * 128 : (h + 1) * 128] for h in range(count)], axis=0)


def unstack_heads(values, count):
    return jnp.concatenate([values[h * ROWS : (h + 1) * ROWS, :] for h in range(count)], axis=1)


def turn(values, cosine, sine):
    return values * cosine + pltpu.roll(values, 64, 1) * sine


def over_heads(table):
    return jnp.concatenate([table] * 8, axis=0)


SCORE_SCALE = HEAD_SIZE ** (-0.5)


def fetch_attention(sources, parts, sem):
    made = []
    for number, (lo, spot) in enumerate(parts):
        cs = pl.ds(lo, spot.shape[-1])
        for core, source in enumerate(sources):

            @pl.when(lax.axis_index("pipe") == core)
            def _(source=source):
                source = source.at[EVERY + (cs,)]
                pltpu.make_async_copy(source, spot, sem.at[number]).start()

        made.append(pltpu.make_async_copy(sources[0].at[EVERY + (cs,)], spot, sem.at[number]))
    return made


EVERY = (slice(None),) * 4


def columns(spot):
    return spot[...].reshape(WIDTH, spot.shape[-1])


def head_gains(gains, layer):
    row = pl.ds(2, 1)
    return gains[layer, row, pl.ds(0, 128)], gains[layer, row, pl.ds(128, 128)]


def attention_forward(layer, state, fetched, parts, gains, tables, branch, normed, qkv, attended):
    q_gain, k_gain = head_gains(gains, layer)
    cos, sin, bias = (table[...] for table in tables)
    rows = state[...].reshape(ROWS, WIDTH).astype(F32)
    normed[...] = (rows * inv_rms(rows) * gains[layer, pl.ds(0, 1), :]).astype(BF)
    fetched[0].wait()
    qkv[...] = dot_nn(normed[...], columns(parts[0][1]))
    query = stack_heads(qkv[:, pl.ds(0, 1024)], 8)
    key = qkv[:, pl.ds(1024, 128)]
    value = qkv[:, pl.ds(1152, 128)].astype(BF)
    q_rot = turn(query * inv_rms(query) * q_gain, over_heads(cos), over_heads(sin)).astype(BF)
    k_rot = turn(key * inv_rms(key) * k_gain, cos, sin).astype(BF)
    scores = dot_nt(q_rot, k_rot) * SCORE_SCALE + over_heads(bias)
    grown = jnp.exp(scores - jnp.max(scores, axis=-1, keepdims=True))
    probs = (grown / jnp.sum(grown, axis=-1, keepdims=True)).astype(BF)
    attended[...] = unstack_heads(dot_nn(probs, value), 8).astype(BF)
    total = None
    for made, (lo, spot) in zip(fetched[1:], parts[1:]):
        made.wait()
        heads = attended[:, pl.ds(lo - QKV, spot.shape[-1])]
        term = dot_nt(heads, columns(spot))
        total = term if total is None else total + term
    branch[...] = total.astype(BF).reshape(RING, OWN, WIDTH)


def attention_backward(layer, d_branch, qkv, fetched, w_out, w_qkv, gains, tables, d_normed, d_qkv, d_gains):
    q_gain, k_gain = head_gains(gains, layer)
    cos, sin, bias = (table[...] for table in tables)
    cos8, sin8 = over_heads(cos), over_heads(sin)
    query = stack_heads(qkv[:, pl.ds(0, 1024)], 8)
    key = qkv[:, pl.ds(1024, 128)]
    value = qkv[:, pl.ds(1152, 128)].astype(BF)
    q_rot = turn(query * inv_rms(query) * q_gain, cos8, sin8).astype(BF)
    k_rot = turn(key * inv_rms(key) * k_gain, cos, sin).astype(BF)
    scores = dot_nt(q_rot, k_rot) * SCORE_SCALE + over_heads(bias)
    grown = jnp.exp(scores - jnp.max(scores, axis=-1, keepdims=True))
    prob = grown / jnp.sum(grown, axis=-1, keepdims=True)
    fetched[0].wait()
    d_att = dot_nn(d_branch[...].reshape(ROWS, WIDTH), columns(w_out)).astype(BF)
    d_att = stack_heads(d_att, 8)
    d_prob = dot_nt(d_att, value)
    d_value = dot_tn(prob.astype(BF), d_att)
    delta = jnp.sum(prob * d_prob, axis=-1, keepdims=True)
    d_scores = (prob * (d_prob - delta)).astype(BF)
    d_q_rot = dot_nn(d_scores, k_rot) * SCORE_SCALE
    d_k_rot = dot_tn(d_scores, q_rot) * SCORE_SCALE
    d_query, q_rows = norm_back(turn(d_q_rot, cos8, -sin8), query, q_gain)
    d_key, k_rows = norm_back(turn(d_k_rot, cos, -sin), key, k_gain)
    d_qkv[:, pl.ds(0, 1024)] = unstack_heads(d_query, 8).astype(BF)
    d_qkv[:, pl.ds(1024, 128)] = d_key.astype(BF)
    d_qkv[:, pl.ds(1152, 128)] = d_value.astype(BF)
    fetched[1].wait()
    made = dot_nt(d_qkv[...], columns(w_qkv))
    d_normed[...] = made.astype(BF).reshape(RING, OWN, WIDTH)
    d_gains[...] = jnp.zeros((8, 128), F32)
    d_gains[pl.ds(0, 1), :] = jnp.sum(q_rows, axis=0, keepdims=True)
    d_gains[pl.ds(1, 1), :] = jnp.sum(k_rows, axis=0, keepdims=True)


def plane_at(chunk, i):
    last = ORDERS[chunk][-1]
    return tuple(i if axis == last else slice(None) for axis in ("z", "x", "y"))


def fetch_experts(place, layer, own, other, dst, sems):
    spots = [dst[0].at[pl.ds(0, 2)], dst[0].at[pl.ds(2, 2)], dst[1]]
    for refs, mine in ((own, True), (other, False)):
        here = place.pipe == layer if mine else place.pipe != layer

        @pl.when(here)
        def _(refs=refs):
            for i, (ref, spot) in enumerate(zip(refs, spots)):
                pltpu.make_async_copy(ref, spot, sems.at[i]).start()

    return [
        pltpu.make_async_copy(ref, spot, sems.at[i]) for i, (ref, spot) in enumerate(zip(own, spots))
    ]


F, T = "f", "t"
FORWARD = (0, 1) * 5 + (
    *(0, 0, 0, 1, 0, 0, 0, 0, 0, 0, 1, 1, 0, 1, 1, 0, 1, 1, 1),
    *(0, 1, 0, 1, 0, 1, 0, 0, 1, 0, 1, 0, 1, 1, 1, 1, 1),
)
BACKWARD_0 = (
    *(0, 1, 0, 1, 0, 0, 1, 1, 0, 0, 0, 0, 1, 0, 1, 1, 0, 0, 0, 0),
    *(1, 1, 1, 0, 0, 1, 1, 1, F, F, 0, F, 1, F, T, F, 0, 1, 0, F),
    *(1, T, F, F, 0, F, 1, F, 0, T, F, 1, 0, T, 1, T, 1, 0, T, 1),
    *(T, 0, F, T, 1, T, 1),
)
BACKWARD_1 = (
    *(0, 0, 0, 1, 1, 0, 1, 1, 0, 0, 0, 0, 0, 1, 0, 1, 0, 0, 0, 0),
    *(1, 1, 1, 1, 0, 0, 1, 1, 1, 1, F, T, F, 0, 1, T, F, 0, F, F),
    *(1, 0, F, 0, 1, 0, T, 1, F, F, 1, F, T, 1, F, 0, T, 1, T, F),
    *(T, 1, T, F, 1, 0, T),
)


def pick_weight(place, rows, lane):
    first = EXPERTS * place.pipe + 2 * (place.at["z"] * RING + place.at["x"])
    column = lax.broadcasted_iota(jnp.int32, rows.shape, 2)
    low = jnp.sum(jnp.where(column == first, rows, 0.0), axis=2, keepdims=True)
    high = jnp.sum(jnp.where(column == first + 1, rows, 0.0), axis=2, keepdims=True)
    return jnp.where(lane < 192, low, high)


def stream_steps(net, place, stream, spread_rows, own, gathered, compute, mix, part, bufs, make, finish, held):
    yield from spread_rows(stream)
    gather = gather_tokens(net, place, stream, own, gathered)
    for _ in range(5):
        next(gather)
        yield
    for chunk in range(3):
        compute(chunk, stream, 0)
    yield
    next(gather)
    yield
    for by in (-1, 1):
        for chunk in range(3):
            compute(chunk, stream, by)
        yield
    together([gather])
    yield
    for chunk in range(3):
        compute(chunk, stream, 2)
    yield
    mix(stream)
    yield
    yield from reduce_tokens(net, place, stream, part, bufs, make)
    finish(stream)
    yield from gather_tensor(net, place, stream, held)


def layer_forward_kernel(layer, *refs):
    refs = list(refs)
    (base, gains, dense), tables, on_core, refs = refs[:3], refs[3:6], refs[6:8], refs[4:]
    gain = gains.at[layer, pl.ds(1, 1)]
    own_w, other_w = refs[4:7], refs[7:10]
    refs = refs[10:]
    if layer == 0:
        attn_1, refs = refs[0], refs[1:]
    out, middle, kept, state = refs[:4]
    results, refs = refs[4:7], refs[7:]
    if layer == 0:
        attn_came, refs = refs[0], refs[1:]
    part, *attn_v, rest_w, attn_sems = refs[:6]
    refs = refs[6:]
    near, refs = state_bufs(refs[:8]), refs[8:]
    (own, held, x_all, part_all, acc, kept_v, hidden, w_in, w_down, spread) = refs[:10]
    *bufs, sems, send, recv = refs[10:]
    bufs = token_bufs(bufs)
    place = Place()
    net = Net(send, recv)
    parts = [
        (0, part_all.at[EVERY + (pl.ds(0, QKV),)]),
        (QKV, part_all.at[EVERY + (pl.ds(QKV, WIDTH - QKV),)]),
        (WIDTH, rest_w),
    ]
    fetched_w = fetch_attention(on_core, parts, attn_sems)

    def attend():
        attention_forward(layer, base, fetched_w, parts, gains, tables, part, *attn_v)

    if layer == 0:
        crossing = net.describe(attn_1, attn_came, place.sibling(), FORWARD_COPIES)
        greet_sibling(place, around(place, "xyz"), attend)

        @pl.when(place.pipe == 1)
        def _():
            crossing.start()

    else:
        greet(around(place, "xyz"), attend)
    fetched = fetch_experts(place, layer, own_w, other_w, (w_in, w_down), sems)
    fetched.append(pltpu.make_async_copy(dense.at[layer], spread, sems.at[5]))
    fetched[-1].start()
    attn_saved = [
        pltpu.make_async_copy(src, dst, attn_sems.at[3 + i])
        for i, (src, dst) in enumerate(zip(attn_v, results))
    ]
    for made in attn_saved:
        made.start()
    z, x, t = place.at["z"], place.at["x"], place.at["y"]

    def clear(i, _):
        acc[lax.div(i, 16), lax.rem(lax.div(i, 4), 4), lax.rem(i, 4)] = jnp.zeros((OWN, 768), F32)
        return 0

    def spread_rows(stream):
        yield from reduce_tensor(net, place, stream, part, near)
        rs = pl.ds(stream * 16, 16)
        value = base[t, rs, :].astype(F32) + near[stream][2][...].astype(F32)
        middle[rs, :] = value
        rounded = (value * inv_rms(value) * gain[...]).astype(BF)
        own[rs, :] = rounded
        x_all[z, x, t, rs, :] = rounded

    def gate_up(chunk, stream, by):
        rs, cs = TILES[chunk, stream].at()
        at = plane_at(chunk, place.step(ORDERS[chunk][-1], by)) + (rs,)
        rows = x_all[at + (cs,)].reshape(256, cs.size)
        made = dot_nt(rows, w_in[:, :, cs].reshape(768, cs.size))
        acc[at] = acc[at] + made.reshape(RING, RING, 16, 768)

    lane = lax.broadcasted_iota(jnp.int32, (RING, 16, HIDDEN), 2)
    saved = [
        pltpu.make_async_copy(x_all, out, sems.at[3]),
        pltpu.make_async_copy(kept_v, kept, sems.at[4]),
    ]

    finished = []

    def mix(stream):
        def tile(i, _):
            at = (lax.div(i, 4), lax.rem(i, 4), slice(None), pl.ds(stream * 16, 16))
            both = acc[at]
            kept_v[at] = both.astype(BF)
            gate, up = both[:, :, :HIDDEN], both[:, :, HIDDEN:]
            weight = pick_weight(place, spread[at], lane)
            hidden[at] = (gate * jax.nn.sigmoid(gate) * up * weight).astype(BF)
            return 0

        lax.fori_loop(0, 16, tile, 0)

    def down(chunk, stream, by):
        rs, cs = TILES[chunk, stream].at()
        at = plane_at(chunk, place.step(ORDERS[chunk][-1], by)) + (rs,)
        made = dot_nn(hidden[at].reshape(256, HIDDEN), w_down[:, :, cs].reshape(HIDDEN, cs.size))
        part_all[at + (cs,)] = made.astype(BF).reshape(RING, RING, 16, cs.size)

    def finish(stream):
        rs = pl.ds(stream * 16, 16)
        held[t, rs, :] = (middle[rs, :] + token_sums(bufs, stream)).astype(BF)
        finished.append(stream)
        if len(finished) == 1:
            for made in saved:
                made.start()

    steps = {
        i: stream_steps(
            net, place, i, spread_rows, own, x_all, gate_up, mix, part_all, bufs, down, finish, held
        )
        for i in range(2)
    }
    for i in range(2):
        next(steps[i])
    lax.fori_loop(0, 64, clear, 0)
    for made in fetched:
        made.wait()
    run_schedule(FORWARD, steps)
    net.finish()
    state[...] = held[...]
    for made in saved + attn_saved:
        made.wait()
    if layer == 0:

        @pl.when(place.pipe == 0)
        def _():
            crossing.wait_recv()

        @pl.when(place.pipe == 1)
        def _():
            crossing.wait_send()


FORWARD_COPIES = 12 + GATHER_COPIES + REDUCE_COPIES + 8


def layer_forward(layer, base, gains, dense, tables, on_core, own_w, other_w, *attn_1):
    outs = [
        jax.ShapeDtypeStruct(TOKENS_ALL, BF),
        jax.ShapeDtypeStruct((OWN, WIDTH), F32),
        jax.ShapeDtypeStruct((RING, RING, RING, OWN, 768), BF),
        jax.ShapeDtypeStruct((RING, OWN, WIDTH), BF),
        jax.ShapeDtypeStruct((ROWS, WIDTH), BF),
        jax.ShapeDtypeStruct((ROWS, QKV), F32),
        jax.ShapeDtypeStruct((ROWS, 1024), BF),
    ]
    kinds = [ANY, VM, ANY, VM, ANY, ANY, ANY]
    if layer == 0:
        outs.append(jax.ShapeDtypeStruct((RING, RING, ROWS, ATT), BF))
        kinds.append(ANY)
    return call(
        functools.partial(layer_forward_kernel, layer),
        1 + 20 * layer,
        outs,
        [Load((RING, OWN, WIDTH), of_pipe if layer == 0 else None), LOAD, ANY, LOAD, LOAD, LOAD]
        + [ANY] * (8 + len(attn_1)),
        kinds,
        [
            VM((RING, OWN, WIDTH), BF),
            VM((ROWS, WIDTH), BF),
            VM((ROWS, QKV), F32),
            VM((ROWS, 1024), BF),
            VM((RING, RING, RING, OWN, ATT - WIDTH), BF),
            pltpu.SemaphoreType.DMA((6,)),
        ]
        + state_scratch()
        + [
            VM((OWN, WIDTH), BF),
            VM((RING, OWN, WIDTH), BF),
            VM(TOKENS_ALL, BF),
            VM(TOKENS_ALL, BF),
            VM((RING, RING, RING, OWN, 768), F32),
            VM((RING, RING, RING, OWN, 768), BF),
            VM((RING, RING, RING, OWN, HIDDEN), BF),
            VM((4, 192, WIDTH), BF),
            VM((2, 192, WIDTH), BF),
            VM((RING, RING, RING, OWN, 128), F32),
        ]
        + token_scratch()
        + [pltpu.SemaphoreType.DMA((6,))],
        (
            base.reshape(*base.shape[:-2], RING, OWN, WIDTH),
            gains,
            dense,
            *tables,
            *on_core,
            *own_w,
            *other_w,
            *attn_1,
        ),
        FORWARD_COPIES + 1,
        60,
    )


def weight_grads(groups, turned):
    for left, lo, right, out in groups:
        turned[...] = left[EVERY + (pl.ds(lo, HIDDEN),)].reshape(2048, HIDDEN).T
        for j in range(4):
            cs = pl.ds(j * 512, 512)
            made = dot_nn(turned[...], right[EVERY + (cs,)].reshape(2048, 512))
            out[pl.ds(lo, HIDDEN), cs] = made.astype(BF)
            yield


def layer_backward_kernel(layer, *refs):
    refs = list(refs)
    if layer == 1:
        given, refs = refs[0], refs[1:]
    else:
        (base, dmid_next, d_branch_next, qkv_next), refs = refs[:4], refs[4:]
        tables, on_core, refs = refs[:3], refs[3:5], refs[5:]
    (middle, gains, dense, kept, tokens) = refs[:5]
    gain, gain_next = gains.at[layer, pl.ds(1, 1)], gains.at[1, pl.ds(0, 1)]
    own_w, other_w = refs[5:8], refs[8:11]
    dmid, d_branch, tally, d_gain = refs[11:15]
    refs = refs[15:]
    if layer == 1:
        (grad_in, grad_down), refs = refs[:2], refs[2:]
    else:
        operands_out, refs = refs[:3], refs[3:]
    if layer == 0:
        (given_out, d_gain_next, d_qkv_out, d_gains_next), refs = refs[:4], refs[4:]
        (part, d_qkv_v, attn_sems), refs = refs[:3], refs[3:]
        near, refs = state_bufs(refs[:8]), refs[8:]
    (own, held, held_d, g_all, x_all, part_all, part_d, acc, both, hidden, w_in, w_down) = refs[:12]
    spread, refs = refs[12], refs[13:]
    if layer == 1:
        (gw_in, gw_down, turned), refs = refs[:3], refs[3:]
    *bufs, sems, send, recv = refs
    tally_bufs = [[bufs.pop(0) for _ in range(4)] for _ in range(3)]
    bufs = token_bufs(bufs)
    place = Place()
    net = Net(send, recv)
    z, x, t = place.at["z"], place.at["x"], place.at["y"]
    d_gain[...] = jnp.zeros((1, WIDTH), F32)
    if layer == 0:
        d_gain_next[...] = jnp.zeros((1, WIDTH), F32)
    mixed, finished = [], []
    attend = None
    if layer == 0:
        w_out = part_all.at[EVERY + (pl.ds(0, 1024),)]
        w_qkv = x_all.at[EVERY + (pl.ds(0, QKV),)]
        fetched_w = fetch_attention(on_core, [(QKV, w_out), (0, w_qkv)], attn_sems)

        def attend():
            attention_backward(
                1,
                d_branch_next,
                qkv_next,
                fetched_w,
                w_out,
                w_qkv,
                gains,
                tables,
                part,
                d_qkv_v,
                d_gains_next,
            )

    greet(around(place, "xyz"), attend)
    fetched = fetch_experts(place, layer, own_w, other_w, (w_in, w_down), sems)
    for src, dst, i in ((kept, both, 3), (dense.at[layer], spread, 7)):
        made = pltpu.make_async_copy(src, dst, sems.at[i])
        made.start()
        fetched.append(made)
    if layer == 1:
        token_copy = pltpu.make_async_copy(tokens, x_all, sems.at[4])
    else:
        saving = pltpu.make_async_copy(d_qkv_v, d_qkv_out, attn_sems.at[2])
        saving.start()
        stores = [
            pltpu.make_async_copy(src, dst, sems.at[4 + i])
            for i, (src, dst) in enumerate(zip((both, hidden, g_all), operands_out))
        ]

    def clear(i, _):
        acc[lax.div(i, 16), lax.rem(lax.div(i, 4), 4), lax.rem(i, 4)] = jnp.zeros((OWN, HIDDEN), F32)
        return 0

    def spread_rows(stream):
        rs = pl.ds(stream * 16, 16)
        if layer == 0:

            def put(t, rs, value):
                own[rs, :] = value

            yield from reduce_tensor(net, place, stream, part, near)
            state_back(place, stream, base, dmid_next, gain_next, near, d_gain_next, put)
        else:
            own[rs, :] = given[t, rs, :]
            yield
            yield
        g_all[z, x, t, rs, :] = own[rs, :]

    def back_hidden(chunk, stream, by):
        rs, cs = TILES[chunk, stream].at()
        at = plane_at(chunk, place.step(ORDERS[chunk][-1], by)) + (rs,)
        rows = g_all[at + (cs,)].reshape(256, cs.size)
        made = dot_nt(rows, w_down[:, :, cs].reshape(HIDDEN, cs.size))
        acc[at] = acc[at] + made.reshape(RING, RING, 16, HIDDEN)

    lane = lax.broadcasted_iota(jnp.int32, (RING, 16, HIDDEN), 2)
    column = lax.broadcasted_iota(jnp.int32, (RING, 16, 128), 2)
    expert = 2 * (z * RING + x)

    def mix(stream):
        def tile(i, _):
            at = (lax.div(i, 4), lax.rem(i, 4), slice(None), pl.ds(stream * 16, 16))
            gate = both[at + (pl.ds(0, HIDDEN),)].astype(F32)
            up = both[at + (pl.ds(HIDDEN, HIDDEN),)].astype(F32)
            d_hidden = acc[at]
            sig = jax.nn.sigmoid(gate)
            silu = gate * sig
            value = silu * up
            dots = value * d_hidden
            low = jnp.sum(jnp.where(lane < 192, dots, 0.0), axis=2, keepdims=True)
            high = jnp.sum(jnp.where(lane < 192, 0.0, dots), axis=2, keepdims=True)
            part_d[at] = (
                jnp.where(column == expert, low, 0.0) + jnp.where(column == expert + 1, high, 0.0)
            ).astype(BF)
            weight = pick_weight(place, spread[at], lane)
            d_hidden = d_hidden * weight
            hidden[at] = (value * weight).astype(BF)
            d_gate = d_hidden * up * sig * (1.0 + gate * (1.0 - sig))
            both[at + (pl.ds(0, HIDDEN),)] = d_gate.astype(BF)
            both[at + (pl.ds(HIDDEN, HIDDEN),)] = (d_hidden * silu).astype(BF)
            return 0

        lax.fori_loop(0, 16, tile, 0)
        mixed.append(stream)
        if layer == 0 and len(mixed) == 2:
            given_out[...] = g_all[z, x]
        if layer == 1 and len(mixed) == 1:
            token_copy.start()

    def back_rows(chunk, stream, by):
        rs, cs = TILES[chunk, stream].at()
        at = plane_at(chunk, place.step(ORDERS[chunk][-1], by)) + (rs,)
        made = dot_nn(both[at].reshape(256, 768), w_in[:, :, cs].reshape(768, cs.size))
        part_all[at + (cs,)] = made.astype(BF).reshape(RING, RING, 16, cs.size)

    def tallying():
        yield from reduce_all(
            net,
            place,
            ("x", "z", "y"),
            ("z", "x", "y"),
            token_block(part_d, TALLY_TILE),
            TALLY_TILE,
            tally_bufs,
        )
        held_d[t, :, :] = tally_bufs[-1][2][...]
        yield from gather_ring(net, place, "y", tensor_blocks(held_d, TALLY_TILE))

    def finish(stream):
        rs = pl.ds(stream * 16, 16)
        back, rows = norm_back(token_sums(bufs, stream), middle[rs, :], gain[...])
        value = own[rs, :].astype(F32) + back
        dmid[rs, :] = value
        held[t, rs, :] = value.astype(BF)
        add_rows(d_gain, rows)
        finished.append(stream)
        if layer == 0 and len(finished) == 1:
            for made in stores:
                made.start()

    steps = {
        i: stream_steps(
            net,
            place,
            i,
            spread_rows,
            own,
            g_all,
            back_hidden,
            mix,
            part_all,
            bufs,
            back_rows,
            finish,
            held,
        )
        for i in range(2)
    }
    for i in range(2):
        next(steps[i])
    lax.fori_loop(0, 64, clear, 0)
    for made in fetched:
        made.wait()
    steps[T] = tallying()
    if layer == 1:

        def fill():
            token_copy.wait()
            yield from weight_grads(
                (
                    (hidden, 0, g_all, gw_down),
                    (both, 0, x_all, gw_in),
                    (both, HIDDEN, x_all, gw_in),
                ),
                turned,
            )

        steps[F] = fill()
        run_schedule(BACKWARD_1, steps)
        stores = []
        for src, dst, i in ((gw_in, grad_in, 5), (gw_down, grad_down, 6)):
            made = pltpu.make_async_copy(src, dst, sems.at[i])
            made.start()
            stores.append(made)
    else:
        run_schedule([step for step in BACKWARD_0 if step != F], steps)
    net.finish()
    d_branch[...] = held[...]
    tally[...] = held_d[...]
    for made in stores:
        made.wait()
    if layer == 0:
        saving.wait()


def layer_backward(layer, lead, middle, gains, dense, kept, tokens, own_w, other_w):
    outs = [
        jax.ShapeDtypeStruct((OWN, WIDTH), F32),
        jax.ShapeDtypeStruct((RING, OWN, WIDTH), BF),
        jax.ShapeDtypeStruct((RING, OWN, 128), BF),
        jax.ShapeDtypeStruct((1, WIDTH), F32),
    ]
    kinds = [VM, VM, VM, VM]
    if layer == 1:
        outs += [
            jax.ShapeDtypeStruct((768, WIDTH), BF),
            jax.ShapeDtypeStruct((HIDDEN, WIDTH), BF),
        ]
        kinds += [ANY, ANY]
    else:
        outs += [
            jax.ShapeDtypeStruct((RING, RING, RING, OWN, 768), BF),
            jax.ShapeDtypeStruct((RING, RING, RING, OWN, HIDDEN), BF),
            jax.ShapeDtypeStruct(TOKENS_ALL, BF),
        ]
        kinds += [ANY, ANY, ANY]
    scratch = []
    lead_kinds = [Load((RING, OWN, WIDTH), of_pipe)]
    if layer == 0:
        lead_kinds = [LOAD] * 7 + [ANY] * 2
    if layer == 0:
        outs += [
            jax.ShapeDtypeStruct((RING, OWN, WIDTH), BF),
            jax.ShapeDtypeStruct((1, WIDTH), F32),
            jax.ShapeDtypeStruct((ROWS, QKV), BF),
            jax.ShapeDtypeStruct((8, 128), F32),
        ]
        kinds += [VM, VM, ANY, VM]
        scratch = [
            VM((RING, OWN, WIDTH), BF),
            VM((ROWS, QKV), BF),
            pltpu.SemaphoreType.DMA((3,)),
        ]
        scratch += state_scratch()
    scratch = scratch + [
        VM((OWN, WIDTH), BF),
        VM((RING, OWN, WIDTH), BF),
        VM((RING, OWN, 128), BF),
        VM(TOKENS_ALL, BF),
        VM(TOKENS_ALL, BF),
        VM(TOKENS_ALL, BF),
        VM((RING, RING, RING, OWN, 128), BF),
        VM((RING, RING, RING, OWN, HIDDEN), F32),
        VM((RING, RING, RING, OWN, 768), BF),
        VM((RING, RING, RING, OWN, HIDDEN), BF),
        VM((4, 192, WIDTH), BF),
        VM((2, 192, WIDTH), BF),
        VM((RING, RING, RING, OWN, 128), F32),
    ]
    if layer == 1:
        scratch += [VM((768, WIDTH), BF), VM((HIDDEN, WIDTH), BF), VM((HIDDEN, 2048), BF)]
    scratch += flat(reduce_scratch(3, TALLY_TILE)) + token_scratch()
    scratch += [pltpu.SemaphoreType.DMA((8,))]
    return call(
        functools.partial(layer_backward_kernel, layer),
        2 + 20 * layer,
        outs,
        lead_kinds + [LOAD] * 2 + [ANY] * 9,
        kinds,
        scratch,
        (
            *lead,
            middle,
            gains,
            dense,
            kept,
            tokens,
            *own_w,
            *other_w,
        ),
        12 + GATHER_COPIES + REDUCE_COPIES + 18 + 8 + 4,
        62,
    )


def body(
    inputs,
    cotangent,
    doc_bounds,
    routes,
    gates,
    norm_attn,
    norm_moe,
    q_gain,
    k_gain,
    w_query,
    key_matrix,
    value_matrix,
    w_out,
    w_gate,
    w_up,
    w_down,
):
    pipe = lax.axis_index("pipe")
    expert = lax.axis_index("expert")
    tensor = lax.axis_index("tensor")
    own_w = (w_gate[0], w_up[0], w_down[0])
    other_w = tuple(lax.ppermute(w, "pipe", [(0, 1), (1, 0)]) for w in own_w)

    named = routes[0][:, :, :, None] == jnp.arange(EXPERTS, dtype=jnp.int32)
    dense = jnp.sum(jnp.where(named, gates[0][:, :, :, None], 0.0), axis=2)
    dense = jnp.concatenate([dense[0], dense[1], jnp.zeros((ROWS, 64), F32)], axis=1)
    dense = dense.reshape(RING, OWN, 128)
    attn_0, attn_1, dense_all, gains, *layout = weight_gather(
        doc_bounds,
        w_query[0],
        key_matrix[0],
        value_matrix[0],
        w_out[0],
        dense,
        norm_attn,
        norm_moe,
        q_gain,
        k_gain,
    )
    first = pipe == 0

    kept, states = [], [inputs]
    by_rows = (RING, RING, RING, OWN, ATT)
    rows_0, rows_1 = attn_0.reshape(by_rows), attn_1.reshape(by_rows)
    weights_of = [(rows_0, rows_0), None]
    for layer in range(2):
        tokens, middle, both, state, normed, qkv, attended, *came = layer_forward(
            layer,
            states[layer],
            gains,
            dense_all,
            layout,
            weights_of[layer],
            own_w,
            other_w,
            *[attn_1][layer:],
        )
        if layer == 0:
            weights_of[1] = (came[0].reshape(by_rows), rows_1)
        kept.append((normed, qkv, attended, middle, tokens, both))
        states.append(state.reshape(ROWS, WIDTH))

    results, gain_sums = [None, None], [None, None]
    d_branch, d_qkv = [None, None], [None, None]
    for layer in (1, 0):
        normed, qkv, attended, middle, tokens, both = kept[layer]
        if layer == 1:
            lead = (cotangent.reshape(2, RING, OWN, WIDTH),)
        else:
            lead = (
                states[1].reshape(RING, OWN, WIDTH),
                dmid,
                d_branch[1],
                kept[1][1],
                *layout,
                *weights_of[1],
            )
        dmid, d_branch[layer], tally, d_norm_m, *more = layer_backward(
            layer, lead, middle, gains, dense_all, both, tokens, own_w, other_w
        )
        results[layer] = [
            normed,
            attended,
            d_branch[layer].reshape(ROWS, WIDTH),
            *more[: 2 * layer],
            states[layer + 1],
            tally.reshape(ROWS, 128),
        ]
        gain_sums[layer] = d_norm_m
    *stored, given_1, gain_1, d_qkv_1, d_gains_1 = more
    results[1].insert(1, d_qkv_1)
    attn_grad, given_0, total, in_came, down_came, act_came, tally_came, given_came, *grads_0 = tail(
        inputs,
        dmid,
        gains,
        d_branch[0],
        kept[0][1],
        layout,
        (gain_sums[0], gain_1, gain_sums[1], d_gains_1),
        weights_of[0],
        results,
        given_1,
        (*stored, kept[0][4]),
    )
    (d_gate, d_up, d_down, acts, givens, d_query, d_key, d_value, d_out, *d_gains) = write_outputs(
        attn_grad,
        total,
        grads_0[0],
        results[1][4],
        in_came,
        grads_0[1],
        results[1][5],
        down_came,
        states[1],
        states[2],
        act_came,
        given_0.reshape(ROWS, WIDTH),
        given_1.reshape(ROWS, WIDTH),
        given_came.reshape(ROWS, WIDTH),
    )
    tally = jnp.where(first, results[0][4], results[1][7])
    tally = jnp.where(first, jnp.stack([tally, tally_came]), jnp.stack([tally_came, tally]))
    tally = tally.astype(F32)[:, :, :EXPERTS]
    d_gates = jnp.sum(jnp.where(named, tally[:, :, None, :], 0.0), axis=3)
    return (
        acts[None],
        givens[None],
        *d_gains,
        d_query[None],
        d_key[None],
        d_value[None],
        d_out[None],
        *(grad.reshape(1, 2, 192, WIDTH) for grad in (d_gate, d_up, d_down)),
        d_gates[None],
    )


def solution(mesh):
    placed = (
        P(None, "expert", None),
        P(None, "expert", None),
        P(None, "expert", None),
        P("pipe", None, "expert", None),
        P("pipe", None, "expert", None),
        P("pipe", None),
        P("pipe", None),
        P("pipe", None),
        P("pipe", None),
        P("pipe", "expert", "tensor"),
        P("pipe", "expert", "tensor"),
        P("pipe", "expert", "tensor"),
        P("pipe", "tensor", "expert"),
        P("pipe", "expert", "tensor", None),
        P("pipe", "expert", "tensor", None),
        P("pipe", "expert", "tensor", None),
    )
    return jax.shard_map(
        body,
        mesh=mesh,
        in_specs=placed,
        out_specs=(
            P("pipe", None, "expert", None),
            P("pipe", None, "expert", None),
            P("pipe", None),
            P("pipe", None),
            P("pipe", None),
            P("pipe", None),
            P("pipe", "expert", "tensor"),
            P("pipe", "expert", "tensor"),
            P("pipe", "expert", "tensor"),
            P("pipe", "tensor", "expert"),
            P("pipe", "expert", "tensor", None),
            P("pipe", "expert", "tensor", None),
            P("pipe", "expert", "tensor", None),
            P("pipe", None, "expert", None),
        ),
        check_vma=False,
    )
```
